512 devices in a mesh: gx: 8 (over z_lo, core), gy: 16 (over y, x), gz: 4 (over z_hi).
Axes of the slice: x: 4, y: 4, z: 16 (z_hi: 4, z_lo: 4; z = z_hi * 4 + z_lo), core: 2. Of those that a mesh axis runs over, the one named last changes fastest.
Arguments:
- right_side: float32 [64, 512, 512], P('gx', 'gy', 'gz'), may hold values from -8 to 8
- predicted: float32 [64, 512, 512], P('gx', 'gy', 'gz'), may hold values from -4 to 4
- zone: int32 [64, 512, 512], P('gx', 'gy', 'gz'), may hold values from 0 to 15
- zone_table: float32 [16], replicated, may hold values from 0.002 to 0.5
Outputs:
- solution_field: float32 [64, 512, 512], P('gx', 'gy', 'gz')
The draws below stay inside these ranges and needn't reach their ends.
All inputs are finite; a program needn't handle non-finite values.
Results may differ from the reference program's by a relative error of at most 0.0001.
Values sent between devices are 32-bit elements; how exact they have to be, the bound alone decides.
No kernel may reach another device: no remote copies, remote signals or barrier semaphores. Data moves between devices by JAX's collectives and lax.ppermute only.
A program may use at most 128 MiB of HBM per device.

```python
import math
import jax
import jax.numpy as jnp

FINE_LEVELS = 2
SMOOTH_DEG = 4
COARSE_DEG = 8
ZONES = 16
NX = 64
NY = 512
NZ = 512


def place_ends(array, own_key, least, largest):
    index_at = [jax.random.randint(jax.random.fold_in(own_key, axis), (), 0, length) for axis, length in enumerate(array.shape)]
    longest = array.shape.index(max(array.shape))
    next_to = index_at[:longest] + [(index_at[longest] + 1) % array.shape[longest]] + index_at[longest + 1:]
    return array.at[tuple(index_at)].set(least).at[tuple(next_to)].set(largest)


def shard_levels(key, shape, shards, low, top_value):
    loudness = 1.0
    for dim, blocks in shards:
        steps = jax.random.uniform(jax.random.fold_in(jax.random.fold_in(key, 6), dim), (blocks,), jnp.float32, low / len(shards), top_value / len(shards))
        loudness = loudness * jnp.repeat(jnp.exp(steps), shape[dim] // blocks).reshape((-1,) + (1,) * (len(shape) - 1 - dim))
    return loudness


def gaussian(key, shape, deviation, most, cuts=(), dtype=jnp.bfloat16):
    values = deviation * jax.random.normal(key, shape, jnp.float32)
    if cuts:
        values = values * shard_levels(key, shape, cuts, -0.22, 0.18)
    return jnp.clip(values, -most, most).astype(dtype)


def setup_inputs(seed: int = 0) -> dict:
    key_list = jax.random.split(jax.random.key(seed), 5)
    right_side = gaussian(key_list[0], (NX, NY, NZ), 1.0, 8.0, ((0, 8), (1, 16), (2, 4)), jnp.float32)
    predicted = gaussian(key_list[1], (NX, NY, NZ), 0.5, 4.0, ((0, 8), (1, 16), (2, 4)), jnp.float32)
    zone = place_ends(jax.random.randint(key_list[2], (NX, NY, NZ), 0, ZONES), jax.random.fold_in(key_list[2], 1), 0, ZONES - 1).astype(jnp.int32)
    zone_table = jnp.clip(jnp.exp(jax.random.uniform(key_list[3], (ZONES,), jnp.float32, math.log(0.002), math.log(0.5))), 0.002, 0.5)
    return {"right_side": right_side, "predicted": predicted, "zone": zone, "zone_table": zone_table}


newmark_shift = 0.0005
smooth_low = 0.5
smooth_high = 2.0
coarse_low = 0.1
coarse_high = 2.0


def lookup(zone, zone_table):
    absorb = jnp.zeros(zone.shape, jnp.float32)
    for code in range(zone_table.shape[0]):
        absorb = absorb + jnp.where(zone == code, zone_table[code], jnp.float32(0.0))
    return absorb


def coarsen(values):
    sx, sy, sz = values.shape
    return values.reshape(sx // 2, 2, sy // 2, 2, sz // 2, 2).sum(axis=(1, 3, 5)) * 0.5


def refine(values):
    return jnp.repeat(jnp.repeat(jnp.repeat(values, 2, axis=0), 2, axis=1), 2, axis=2)


def zero_padder(field):
    return jnp.pad(field, 1)


def operate(field, diagonal, padder):
    padded = padder(field)
    beside = padded[2:, 1:-1, 1:-1] + padded[:-2, 1:-1, 1:-1]
    beside = beside + padded[1:-1, 2:, 1:-1] + padded[1:-1, :-2, 1:-1]
    beside = beside + padded[1:-1, 1:-1, 2:] + padded[1:-1, 1:-1, :-2]
    return diagonal * field - beside


def chebyshev(field, source, diagonal, padder, degree, low, high, start_zero):
    centre_value = (high + low) / 2.0
    half_width = (high - low) / 2.0
    ratio_value = centre_value / half_width
    factor = 1.0 / ratio_value
    if start_zero:
        scaled = source / diagonal
    else:
        scaled = (source - operate(field, diagonal, padder)) / diagonal
    update = scaled / centre_value
    field = field + update
    for sweep in range(1, degree):
        scaled = (source - operate(field, diagonal, padder)) / diagonal
        factor_next = 1.0 / (2.0 * ratio_value - factor)
        update = (factor_next * factor) * update + (2.0 * factor_next / half_width) * scaled
        field = field + update
        factor = factor_next
    return field


def reference(right_side, predicted, zone, zone_table):
    masses = [newmark_shift + lookup(zone, zone_table)]
    for depth in range(FINE_LEVELS):
        masses.append(coarsen(masses[-1]))
    smoothed = []
    sources = []
    source = right_side
    field = predicted
    for depth in range(FINE_LEVELS):
        diagonal = 6.0 + masses[depth]
        field = chebyshev(field, source, diagonal, zero_padder, SMOOTH_DEG, smooth_low, smooth_high, depth > 0)
        residual = source - operate(field, diagonal, zero_padder)
        smoothed.append(field)
        sources.append(source)
        source = coarsen(residual)
        field = jnp.zeros_like(source)
    correction = chebyshev(jnp.zeros_like(source), source, 6.0 + masses[FINE_LEVELS], zero_padder, COARSE_DEG, coarse_low, coarse_high, True)
    for depth in reversed(range(FINE_LEVELS)):
        field = smoothed[depth] + refine(correction)
        correction = chebyshev(field, sources[depth], 6.0 + masses[depth], zero_padder, SMOOTH_DEG, smooth_low, smooth_high, False)
    return correction
```

```python
import jax
import jax.numpy as jnp
from jax import lax
from jax.experimental import pallas as pl
from jax.experimental.pallas import tpu as pltpu
from jax.sharding import PartitionSpec as P

SMOOTH_DEG = 4
COARSE_DEG = 8
SHIFT = 0.0005
SMOOTH = (0.5, 2.0)
COARSE = (0.1, 2.0)
F32 = jnp.float32
HIGHEST = lax.Precision.HIGHEST


def factors(degree, low, high):
    centre, half = (high + low) / 2.0, (high - low) / 2.0
    ratio = centre / half
    factor = 1.0 / ratio
    pairs = [(0.0, 1.0 / centre)]
    for _ in range(1, degree):
        following = 1.0 / (2.0 * ratio - factor)
        pairs.append((following * factor, 2.0 * following / half))
        factor = following
    return pairs


def lanes_like(shape):
    return lax.broadcasted_iota(jnp.int32, shape, len(shape) - 1)


def rows_like(shape):
    return lax.broadcasted_iota(jnp.int32, shape, len(shape) - 2)


def turn(v, by, axis):
    by = by % v.shape[axis]
    return v if by == 0 else pltpu.roll(v, by, axis)


def across(own, lane):
    up = [turn(v, 1, 1) for v in own]
    down = [turn(v, -1, 1) for v in own]
    if len(own) == 2:
        up = [jnp.where(lane == 0, up[1 - h], up[h]) for h in range(2)]
        down = [jnp.where(lane == 127, down[1 - h], down[h]) for h in range(2)]
    return [p + q for p, q in zip(up, down)]


def put(x, i, h, row, value, height, cyclic):
    x[i, h, pl.ds(8 + row, 8)] = value
    if cyclic and row == 0:
        x[i, h, pl.ds(8 + height, 1)] = value[0:1]
    if cyclic and row == height - 8:
        x[i, h, pl.ds(7, 1)] = value[7:8]


def stencil(x, first, group, halves, rows, use):
    lane = lanes_like((8, 128))
    for row in rows:
        def load(i):
            return [x[i, h, pl.ds(8 + row, 8)] for h in range(halves)]

        below, own = load(first - 1), load(first)
        for j in range(group):
            i = first + j
            above = load(i + 1)
            side = across(own, lane)
            total = [
                (below[h] + above[h]) + (x[i, h, pl.ds(7 + row, 8)] + x[i, h, pl.ds(9 + row, 8)]) + side[h]
                for h in range(halves)
            ]
            use(j, row, own, total)
            below, own = own, above


def sweep(xin, xout, upd, src, inv, start, stop, a, c, group, cyclic, offset=0):
    halves, height = src.shape[1], src.shape[2]

    def body(first):
        def use(j, row, own, total):
            i, tile = first + j, pl.ds(row, 8)
            for h in range(halves):
                g = (src[i + offset, h, tile] + total[h]) * inv[i + offset, h, tile] - own[h]
                u = c * g if a == 0.0 else a * upd[i, h, tile] + c * g
                upd[i, h, tile] = u
                put(xout, i, h, row, own[h] + u, height, cyclic)

        stencil(xin, first, group, halves, range(0, height, 8), use)

    steps = (stop - start) // group
    if steps == 1:
        body(start)
    else:
        def step(n, carry):
            body(start + n * group)
            return carry

        lax.fori_loop(0, steps, step, 0)


def dot(a, b):
    return lax.dot_general(a, b, (((1,), (0,)), ((), ())), precision=HIGHEST, preferred_element_type=F32)


def inverse(mass):
    return jnp.where(mass > 0.0, 1.0 / (6.0 + mass), 0.0)


def first_kernel(table, pred, right, zone, main, to_next, to_before, codes, sems):
    moves = ((zone, codes), (pred, main.at[0]), (right, main.at[1]))
    copies = [pltpu.make_async_copy(*move, sems.at[n]) for n, move in enumerate(moves)]
    for copy in copies:
        copy.start()
    copies[0].wait()
    lane = lanes_like((32, 128))
    for x in range(8):
        code = codes[x]
        absorb = jnp.zeros((32, 128), F32)
        for k in range(16):
            absorb = absorb + jnp.where(code == k, table[k], 0.0)
        main[2, x] = SHIFT + absorb
    copies[1].wait()
    copies[2].wait()
    for edge, out in ((120, to_next), (0, to_before)):
        for half, fields in ((0, (0, 1)), (1, (2,))):
            packed = jnp.zeros((32, 128), F32)
            for n, f in enumerate(fields):
                for x in range(8):
                    at = 64 * n + 8 * x
                    moved = turn(main[f, x], at - edge, 1)
                    packed = jnp.where((lane >= at) & (lane < at + 8), moved, packed)
            out[half] = packed


def second_kernel(main, zbefore, znext, to_next, to_before):
    for start, out in ((24, to_next), (0, to_before)):
        rows = pl.ds(start, 8)
        for f in range(3):
            for x in range(8):
                out[f * 8 + x] = main[f, x, rows]
        for half in range(2):
            out[24 + half] = zbefore[half, rows]
            out[26 + half] = znext[half, rows]


def main_tile(f, k, t):
    return 4 * k + t + (f > 0) * (32 + 28 * (f - 1))


def y_tile(f, k):
    return 88 + 10 * f + (2 * k if k < 3 else 3 + k)


TILES = 142


def third_kernel(main, zbefore, znext, ybefore, ynext, to_next, to_before):
    row = rows_like((8, 128))
    for out in (to_next, to_before):
        for k in range(8):
            x = 7 - k if out is to_next else k
            for f in range(3 if k < 7 else 1):
                for t in range(4):
                    out[main_tile(f, k, t)] = main[f, x, pl.ds(8 * t, 8)]
                n, at = f * 8 + x, y_tile(f, k)
                if k < 3:
                    out[at] = ynext[n]
                    out[at + 1] = ybefore[n]
                elif k < 7:
                    out[at] = jnp.where(row < 4, ynext[n], ybefore[n])
        for half in range(2):
            for t in range(4):
                out[118 + half * 4 + t] = zbefore[half, pl.ds(8 * t, 8)]
                out[126 + half * 4 + t] = znext[half, pl.ds(8 * t, 8)]
        out[134:138] = ynext[24:28]
        out[138:142] = ybefore[24:28]


def coarsen_matrix(source):
    rows = lax.broadcasted_iota(jnp.int32, (128, 128), 0)
    cols = lax.broadcasted_iota(jnp.int32, (128, 128), 1)
    return jnp.where(source(rows) == cols, 0.5, 0.0).astype(F32)


def descend_kernel(main, zbefore, znext, ybefore, ynext, before, after, fa, src, inv, one_out, to_next, to_before,
                   fb, upd, mass, pair):
    lane = lanes_like((8, 128))
    row = rows_like((8, 128))
    zero = jnp.zeros((8, 128), F32)

    def own_tile(f, x, t):
        half = f // 2
        if 1 <= t < 5:
            tile = pl.ds(8 * t - 8, 8)
            return main[f, x, tile], zbefore[half, tile], znext[half, tile]
        side = ynext if t == 5 else ybefore
        return side[f * 8 + x], side[24 + half], side[26 + half]

    def far_tile(message, f, k, t):
        half = f // 2
        if 1 <= t < 5:
            return message[main_tile(f, k, t - 1)], message[118 + half * 4 + t - 1], message[126 + half * 4 + t - 1]
        at, corner = y_tile(f, k), 134 if t == 5 else 138
        if k < 3:
            centre = message[at + (t == 0)]
        elif k < 7:
            centre = jnp.where((row < 4) == (t == 5), message[at], 0.0)
        else:
            centre = zero
        return centre, message[corner + half], message[corner + 2 + half]

    for plane in range(24):
        x = plane % 8
        for h in range(2):
            for field in (fa, fb):
                field[plane, h, pl.ds(0, 8)] = zero
                field[plane, h, pl.ds(56, 8)] = zero
        for f in range(3 if 0 < plane < 23 else 1):
            at = (f % 2) * 64 + 8 * x
            for t in range(6):
                if plane < 8:
                    centre, zb, zn = far_tile(before, f, 7 - x, t)
                elif plane < 16:
                    centre, zb, zn = own_tile(f, x, t)
                else:
                    centre, zb, zn = far_tile(after, f, x, t)
                side = jnp.where(lane < 8, turn(zn, -at, 1), 0.0)
                side = jnp.where(lane >= 120, turn(zb, 120 - at, 1), side)
                if f == 2:
                    if 8 <= plane < 16 and 1 <= t < 5:
                        mass[x, pl.ds(8 * t - 8, 8)] = centre
                    centre, side = inverse(centre), inverse(side)
                dest, down = ((fa, 8), (src, 0), (inv, 0))[f]
                dest[plane, 0, pl.ds(8 * t + down, 8)] = centre
                dest[plane, 1, pl.ds(8 * t + down, 8)] = side
    xin, xout = fa, fb
    for k, (a, c) in enumerate(factors(SMOOTH_DEG, *SMOOTH)):
        sweep(xin, xout, upd, src, inv, k + 1, 23 - k, a, c, 2, False)
        xin, xout = xout, xin
    def residual(j, row, own_tile, total):
        if 8 <= row < 40:
            tile = pl.ds(row - 8, 8)
            res = (src[8 + j, 0, pl.ds(row, 8)] + total[0]) - (6.0 + mass[j, tile]) * own_tile[0]
            if j % 2 == 0:
                held[row] = res
            else:
                pair[j // 2, tile] = held[row] + res
                pair[4 + j // 2, tile] = mass[j - 1, tile] + mass[j, tile]

    held = {}
    stencil(xin, 8, 8, 2, range(8, 40, 8), residual)
    even = pair[:, pl.ds(0, 16, stride=2), :] + pair[:, pl.ds(1, 16, stride=2), :]
    one = dot(even.reshape(128, 128), coarsen_matrix(lambda r: r // 2)).reshape(2, 4, 16, 128)
    one_out[...] = one
    lane = lanes_like((16, 128))
    for edge, out in ((32, to_next), (0, to_before)):
        for f in range(2):
            packed = jnp.zeros((16, 128), F32)
            for i in range(4):
                packed = jnp.where(lane // 32 == i, turn(one[f, i], 32 * i - edge, 1), packed)
            out[f] = packed


def widen_kernel(one, zbefore, znext, out):
    lane = lanes_like((16, 128))
    for f in range(2):
        for i in range(4):
            v = one[f, i]
            v = jnp.where(lane // 32 == 2, turn(znext[f], 64 - 32 * i, 1), v)
            out[0, f, i] = jnp.where(lane // 32 == 3, turn(zbefore[f], 96 - 32 * i, 1), v)


def rows_kernel(near, to_next, to_before):
    for start, extra, out in ((8, 7, to_next), (0, 8, to_before)):
        for n in range(32):
            block = near.at[n // 4 % 4, n // 16, n % 4]
            out[n] = block[pl.ds(start, 8)]
            out[32 + n // 8, pl.ds(n % 8, 1)] = block[pl.ds(extra, 1)]


def join_kernel(near, ybefore, ynext, out):
    row = rows_like((8, 128))
    for n in range(32):
        place = n // 4 % 4, n // 16, n % 4
        tile, at = 32 + n // 8, pl.ds(n % 8, 1)
        out[(*place, pl.ds(0, 16))] = near[place]
        out[(*place, pl.ds(16, 8))] = ynext[n]
        mix = jnp.where(row == 0, ynext[tile, at], 0.0)
        out[(*place, pl.ds(24, 8))] = jnp.where(row == 7, ybefore[tile, at], mix)
        out[(*place, pl.ds(32, 8))] = ybefore[n]


def middle_kernel(place, near, far, fb, src, inv, two_out, to_next, to_before,
                  fa, upd, mass, pair, pairs):
    zero = jnp.zeros((40, 128), F32)
    for end in (0, 1, 2, 3, 4, 5, 6, 39, 40, 41, 42, 43, 44, 45, 46):
        for field in (fa, fb):
            field[end, 0, pl.ds(8, 40)] = zero
        src[end, 0] = zero
        inv[end, 0] = zero
    (_, scale), *later = factors(SMOOTH_DEG, *SMOOTH)
    for j in range(8):
        group = place[0] ^ ((j & 1) * 4 + (j >> 1 & 1) * 2 + (j >> 2))
        for i in range(4):
            plane = 7 + 4 * group + i
            values = [(near if j < 4 else far)[j % 4, f, i] for f in range(2)]
            mass[plane] = values[1]
            values[1] = inverse(values[1])
            src[plane, 0] = values[0]
            inv[plane, 0] = values[1]
            u = scale * (values[0] * values[1])
            upd[plane, 0] = u
            for t in range(5):
                put(fa, plane, 0, 8 * t, u[8 * t:8 * t + 8], 40, True)
    xin, xout = fa, fb
    for a, c in later:
        sweep(xin, xout, upd, src, inv, 7, 39, a, c, 4, True)
        xin, xout = xout, xin

    def step(n, carry):
        def residual(j, row, own, total):
            p, tile = 7 + 4 * n + j, pl.ds(row, 8)
            res = (src[p, 0, tile] + total[0]) - (6.0 + mass[p, tile]) * own[0]
            if j % 2 == 0:
                held[row] = res
            else:
                pair[2 * n + j // 2, tile] = held[row] + res
                pair[16 + 2 * n + j // 2, tile] = mass[p - 1, tile] + mass[p, tile]

        held = {}
        stencil(xin, 7 + 4 * n, 4, 1, range(0, 40, 8), residual)
        return carry

    lax.fori_loop(0, 8, step, 0)
    even = pair[:, pl.ds(0, 20, stride=2), :] + pair[:, pl.ds(1, 20, stride=2), :]
    pairs[:, pl.ds(0, 20)] = even
    pairs[:, pl.ds(20, 4)] = jnp.zeros((32, 4, 128), F32)
    down = [coarsen_matrix(lambda r, h=h: 64 * h + 16 + jnp.where(r < 96, r // 2, r // 2 - 64)) for h in range(2)]
    for f in range(2):
        low = pairs[pl.ds(16 * f, 8)].reshape(192, 128)
        high = pairs[pl.ds(16 * f + 8, 8)].reshape(192, 128)
        made = (dot(low, down[0]) + dot(high, down[1])).reshape(8, 24, 128)
        for i in range(8):
            n = 8 * f + i
            two_out[n] = made[i, 0:8]
            at = pl.ds(2 * (n % 4), 2)
            to_next[n] = made[i, 0:8]
            to_before[n] = made[i, 0:8]
            to_next[16 + n // 4, at] = made[i, 18:20]
            to_before[16 + n // 4, at] = made[i, 8:10]


def one_hot(shape, axis, source):
    at = lax.broadcasted_iota(jnp.int32, shape, axis)
    return jnp.where(at == source, 1.0, 0.0).astype(F32)


def ascend_kernel(place, two, before, after, x1, src1, inv1, x0, src0, inv0, out,
                  ca, cb, cupd, csrc, cinv, flat, oa, ob, oupd, za, zb, zupd):
    row = rows_like((8, 128))
    lane = lanes_like((32, 128))
    (_, scale), *later = factors(COARSE_DEG, *COARSE)
    for i in range(8):
        values = []
        for f in range(2):
            n = 8 * f + i
            mix = jnp.where(row < 2, turn(after[16 + n // 4], -2 * (n % 4), 0), 0.0)
            mix = jnp.where(row >= 6, turn(before[16 + n // 4], 6 - 2 * (n % 4), 0), mix)
            values.append(jnp.concatenate([two[n], after[n], mix, before[n]], axis=0))
        values[1] = inverse(values[1])
        csrc[1 + i, 0] = values[0]
        cinv[1 + i, 0] = values[1]
        u = scale * (values[0] * values[1])
        cupd[1 + i, 0] = u
        for t in range(4):
            put(ca, 1 + i, 0, 8 * t, u[8 * t:8 * t + 8], 32, True)
    xin, xout = ca, cb
    core = pl.ds(8, 32)
    for a, c in later:
        xin[0, 0, core] = jnp.where(lane >= 64, pltpu.roll(xin[8, 0, core], 64, 1), 0.0)
        xin[9, 0, core] = jnp.where(lane < 64, pltpu.roll(xin[1, 0, core], 64, 1), 0.0)
        sweep(xin, xout, cupd, csrc, cinv, 1, 9, a, c, 8, True)
        xin, xout = xout, xin
    zero = jnp.zeros((32, 128), F32)
    for end in (0, 1, 2, 19, 20, 21):
        flat[end] = zero
    for q in range(16):
        v = xin[1 + q % 8, 0, core]
        flat[3 + q] = v if q < 8 else pltpu.roll(v, 64, 1)
    l = lax.broadcasted_iota(jnp.int32, (1, 128), 1)
    wide = one_hot((128, 128), 0, jnp.where(l < 96, 16 + l // 2, l // 2 - 48))
    r = lax.broadcasted_iota(jnp.int32, (40, 1), 0)
    tall = one_hot((40, 32), 1, jnp.where(r < 28, r // 2, 12 + r // 2))
    part = dot(flat[pl.ds(2 * place[0], 8)].reshape(256, 128), wide)
    fine = dot(tall, jnp.concatenate([part[32 * w:32 * w + 32] for w in range(8)], axis=1))
    first = 4 * place[0] + 1
    for w in range(16):
        v = w // 2
        for t in range(5):
            value = x1[first + w, 0, pl.ds(8 + 8 * t, 8)] + fine[8 * t:8 * t + 8, 128 * v:128 * v + 128]
            put(oa, w, 0, 8 * t, value, 40, True)
    xin, xout = oa, ob
    for k, (a, c) in enumerate(factors(SMOOTH_DEG, *SMOOTH)):
        sweep(xin, xout, oupd, src1, inv1, k + 1, 15 - k, a, c, 14 - 2 * k, True, offset=first)
        xin, xout = xout, xin
    side = jnp.where((l < 8) | (l >= 120), 64 + l // 2, -1)
    wide = [one_hot((128, 128), 0, l // 2), one_hot((128, 128), 0, side)]
    r = lax.broadcasted_iota(jnp.int32, (48, 1), 0)
    tall = one_hot((48, 40), 1, jnp.where(r < 8, 36 + r // 2, r // 2 - 4))
    below = xin[4:12, 0, 8:48].reshape(320, 128)
    zero = jnp.zeros((8, 128), F32)
    for h in range(2):
        part = dot(below, wide[h])
        fine = dot(tall, jnp.concatenate([part[40 * w:40 * w + 40] for w in range(8)], axis=1))
        for w in range(16):
            v = w // 2
            za[w, h, pl.ds(8, 48)] = x0[4 + w, h, pl.ds(8, 48)] + fine[:, 128 * v:128 * v + 128]
            for field in (za, zb):
                field[w, h, pl.ds(0, 8)] = zero
                field[w, h, pl.ds(56, 8)] = zero
    xin, xout = za, zb
    for k, (a, c) in enumerate(factors(SMOOTH_DEG, *SMOOTH)):
        sweep(xin, xout, zupd, src0, inv0, k + 1, 15 - k, a, c, 2, False, offset=4)
        xin, xout = xout, xin
    out[...] = xin[4:12, 0, 16:48]


def call(kernel, outs, scratch, *args, spaces=(), limit=24):
    vmem = pl.BlockSpec(memory_space=pltpu.VMEM)
    spaces = [pl.BlockSpec(memory_space=space) for space in spaces]
    scratch = [pltpu.VMEM(s, F32) if isinstance(s, tuple) else s for s in scratch]
    return pl.pallas_call(
        kernel,
        out_shape=[jax.ShapeDtypeStruct(s, F32) for s in outs],
        in_specs=spaces + [vmem] * (len(args) - len(spaces)),
        out_specs=[vmem] * len(outs),
        scratch_shapes=scratch,
        compiler_params=pltpu.CompilerParams(vmem_limit_bytes=limit * 1024 * 1024),
    )(*args)


def shift(value, axis, by):
    count = lax.axis_size(axis)
    pairs = [(i, i + by) for i in range(count) if 0 <= i + by < count]
    return lax.ppermute(value, axis, pairs)


def swap(value, axis, bit):
    return lax.ppermute(value, axis, [(i, i ^ bit) for i in range(lax.axis_size(axis))])


def per_device(right_side, predicted, zone, zone_table):
    place = lax.axis_index("gx").astype(jnp.int32).reshape(1)
    block = (8, 32, 128)
    main, nxt, bef = call(first_kernel, [(3, *block), (2, 32, 128), (2, 32, 128)],
                          [pltpu.VMEM(block, jnp.int32), pltpu.SemaphoreType.DMA((3,))],
                          zone_table, predicted, right_side, zone,
                          spaces=[pltpu.SMEM, pltpu.HBM, pltpu.HBM, pltpu.HBM], limit=56)
    zbefore, znext = shift(nxt, "gz", 1), shift(bef, "gz", -1)
    nxt, bef = call(second_kernel, [(28, 8, 128)] * 2, [], main, zbefore, znext)
    ybefore, ynext = shift(nxt, "gy", 1), shift(bef, "gy", -1)
    nxt, bef = call(third_kernel, [(TILES, 8, 128)] * 2, [], main, zbefore, znext, ybefore, ynext)
    before, after = shift(nxt, "gx", 1), shift(bef, "gx", -1)
    tall, flat = (24, 2, 64, 128), (24, 2, 48, 128)
    x0, src0, inv0, one, nxt, bef = call(
        descend_kernel,
        [tall, flat, flat, (2, 4, 16, 128), (2, 16, 128), (2, 16, 128)],
        [tall, flat, block, block],
        main, zbefore, znext, ybefore, ynext, before, after)
    zbefore, znext = shift(nxt, "gz", 1), shift(bef, "gz", -1)
    near, = call(widen_kernel, [(1, 2, 4, 16, 128)], [], one, zbefore, znext)
    near = jnp.concatenate([near, swap(near, "gx", 4)])
    near = jnp.concatenate([near, swap(near, "gx", 2)])
    nxt, bef = call(rows_kernel, [(36, 8, 128)] * 2, [], near)
    ybefore, ynext = shift(nxt, "gy", 1), shift(bef, "gy", -1)
    near, = call(join_kernel, [(4, 2, 4, 40, 128)], [], near, ybefore, ynext)
    far = swap(near, "gx", 1)
    tall, flat = (47, 1, 56, 128), (47, 1, 40, 128)
    x1, src1, inv1, two, nxt, bef = call(
        middle_kernel,
        [tall, flat, flat, (16, 8, 128), (20, 8, 128), (20, 8, 128)],
        [tall, flat, (47, 40, 128), (32, 40, 128), (32, 24, 128)],
        place, near, far, spaces=[pltpu.SMEM])
    before, after = shift(nxt, "gy", 1), shift(bef, "gy", -1)
    out, = call(
        ascend_kernel,
        [(8, 32, 128)],
        [(10, 1, 48, 128)] * 2 + [(10, 1, 32, 128)] * 3 + [(22, 32, 128)]
        + [(16, 1, 56, 128)] * 2 + [(16, 1, 40, 128)] + [(16, 2, 64, 128)] * 2 + [(16, 2, 48, 128)],
        place, two, before, after, x1, src1, inv1, x0, src0, inv0, spaces=[pltpu.SMEM])
    return out


def solution(mesh):
    placed = (P("gx", "gy", "gz"), P("gx", "gy", "gz"), P("gx", "gy", "gz"), P())
    return jax.shard_map(
        per_device, mesh=mesh, in_specs=placed, out_specs=P("gx", "gy", "gz"), check_vma=False
    )
```

```python
import jax
import jax.numpy as jnp
from jax import lax
from jax.experimental import pallas as pl
from jax.experimental.pallas import tpu as pltpu
from jax.sharding import PartitionSpec as P

SMOOTH_DEG = 4
COARSE_DEG = 8
SHIFT = 0.0005
SMOOTH = (0.5, 2.0)
COARSE = (0.1, 2.0)
F32 = jnp.float32
HIGHEST = lax.Precision.HIGHEST


def factors(degree, low, high):
    centre, half = (high + low) / 2.0, (high - low) / 2.0
    ratio = centre / half
    factor = 1.0 / ratio
    pairs = [(0.0, 1.0 / centre)]
    for _ in range(1, degree):
        following = 1.0 / (2.0 * ratio - factor)
        pairs.append((following * factor, 2.0 * following / half))
        factor = following
    return pairs


def lanes_like(shape):
    return lax.broadcasted_iota(jnp.int32, shape, len(shape) - 1)


def rows_like(shape):
    return lax.broadcasted_iota(jnp.int32, shape, len(shape) - 2)


def turn(v, by, axis):
    by = by % v.shape[axis]
    return v if by == 0 else pltpu.roll(v, by, axis)


def across(own, lane):
    up = [turn(v, 1, 1) for v in own]
    down = [turn(v, -1, 1) for v in own]
    if len(own) == 2:
        up = [jnp.where(lane == 0, up[1 - h], up[h]) for h in range(2)]
        down = [jnp.where(lane == 127, down[1 - h], down[h]) for h in range(2)]
    return [p + q for p, q in zip(up, down)]


def put(x, i, h, row, value, height, cyclic):
    x[i, h, pl.ds(8 + row, 8)] = value
    if cyclic and row == 0:
        x[i, h, pl.ds(8 + height, 1)] = value[0:1]
    if cyclic and row == height - 8:
        x[i, h, pl.ds(7, 1)] = value[7:8]


def stencil(x, first, group, halves, rows, use):
    lane = lanes_like((8, 128))
    for row in rows:
        def load(i):
            return [x[i, h, pl.ds(8 + row, 8)] for h in range(halves)]

        below, own = load(first - 1), load(first)
        for j in range(group):
            i = first + j
            above = load(i + 1)
            side = across(own, lane)
            total = [
                (below[h] + above[h]) + (x[i, h, pl.ds(7 + row, 8)] + x[i, h, pl.ds(9 + row, 8)]) + side[h]
                for h in range(halves)
            ]
            use(j, row, own, total)
            below, own = own, above


def sweep(xin, xout, upd, src, inv, start, stop, a, c, group, cyclic, offset=0):
    halves, height = src.shape[1], src.shape[2]

    def body(first):
        def use(j, row, own, total):
            i, tile = first + j, pl.ds(row, 8)
            for h in range(halves):
                g = (src[i + offset, h, tile] + total[h]) * inv[i + offset, h, tile] - own[h]
                u = c * g if a == 0.0 else a * upd[i, h, tile] + c * g
                upd[i, h, tile] = u
                put(xout, i, h, row, own[h] + u, height, cyclic)

        stencil(xin, first, group, halves, range(0, height, 8), use)

    steps = (stop - start) // group
    if steps == 1:
        body(start)
    else:
        def step(n, carry):
            body(start + n * group)
            return carry

        lax.fori_loop(0, steps, step, 0)


def dot(a, b):
    return lax.dot_general(a, b, (((1,), (0,)), ((), ())), precision=HIGHEST, preferred_element_type=F32)


def inverse(mass):
    return jnp.where(mass > 0.0, 1.0 / (6.0 + mass), 0.0)


def by_parity(place, a, b, body):
    odd = place[0] % 2
    pl.when(odd == 1)(lambda: body(a, b))
    pl.when(odd == 0)(lambda: body(b, a))


def first_kernel(table, pred, right, zone, main, to_next, to_before, codes, sems):
    moves = ((zone, codes), (pred, main.at[0]), (right, main.at[1]))
    copies = [pltpu.make_async_copy(*move, sems.at[n]) for n, move in enumerate(moves)]
    for copy in copies:
        copy.start()
    copies[0].wait()
    lane = lanes_like((32, 128))
    for x in range(8):
        code = codes[x]
        absorb = jnp.zeros((32, 128), F32)
        for k in range(16):
            absorb = absorb + jnp.where(code == k, table[k], 0.0)
        main[2, x] = SHIFT + absorb
    copies[1].wait()
    copies[2].wait()
    for edge, out in ((120, to_next), (0, to_before)):
        for half, fields in ((0, (0, 1)), (1, (2,))):
            packed = jnp.zeros((32, 128), F32)
            for n, f in enumerate(fields):
                for x in range(8):
                    at = 64 * n + 8 * x
                    moved = turn(main[f, x], at - edge, 1)
                    packed = jnp.where((lane >= at) & (lane < at + 8), moved, packed)
            out[half] = packed


def second_kernel(py, main, zbefore, znext, ya, yb, kept):
    kept[...] = main[...]

    def body(to_next, to_before):
        for start, out in ((24, to_next), (0, to_before)):
            rows = pl.ds(start, 8)
            for f in range(3):
                for x in range(8):
                    out[f * 8 + x] = main[f, x, rows]
            for half in range(2):
                out[24 + half] = zbefore[half, rows]
                out[26 + half] = znext[half, rows]

    by_parity(py, ya, yb, body)


def main_tile(f, k, t):
    return 4 * k + t + (f > 0) * (32 + 28 * (f - 1))


def y_tile(f, k):
    return 88 + 10 * f + (2 * k if k < 3 else 3 + k)


TILES = 142


def third_kernel(px, py, main, zbefore, znext, ya, yb, xa, xb, ybefore, ynext):
    row = rows_like((8, 128))

    def settle(after, before):
        ynext[...] = after[...]
        ybefore[...] = before[...]

    by_parity(py, ya, yb, settle)

    def body(to_next, to_before):
        for out in (to_next, to_before):
            for k in range(8):
                x = 7 - k if out is to_next else k
                for f in range(3 if k < 7 else 1):
                    for t in range(4):
                        out[main_tile(f, k, t)] = main[f, x, pl.ds(8 * t, 8)]
                    n, at = f * 8 + x, y_tile(f, k)
                    if k < 3:
                        out[at] = ynext[n]
                        out[at + 1] = ybefore[n]
                    elif k < 7:
                        out[at] = jnp.where(row < 4, ynext[n], ybefore[n])
            for half in range(2):
                for t in range(4):
                    out[118 + half * 4 + t] = zbefore[half, pl.ds(8 * t, 8)]
                    out[126 + half * 4 + t] = znext[half, pl.ds(8 * t, 8)]
            out[134:138] = ynext[24:28]
            out[138:142] = ybefore[24:28]

    by_parity(px, xa, xb, body)


def coarsen_matrix(source):
    rows = lax.broadcasted_iota(jnp.int32, (128, 128), 0)
    cols = lax.broadcasted_iota(jnp.int32, (128, 128), 1)
    return jnp.where(source(rows) == cols, 0.5, 0.0).astype(F32)


def descend_kernel(px, main, zbefore, znext, ybefore, ynext, xa, xb, fa, src, inv, one_out, to_next, to_before,
                   fb, upd, mass, pair):
    lane = lanes_like((8, 128))
    row = rows_like((8, 128))
    zero = jnp.zeros((8, 128), F32)

    def own_tile(f, x, t):
        half = f // 2
        if 1 <= t < 5:
            tile = pl.ds(8 * t - 8, 8)
            return main[f, x, tile], zbefore[half, tile], znext[half, tile]
        side = ynext if t == 5 else ybefore
        return side[f * 8 + x], side[24 + half], side[26 + half]

    def far_tile(message, f, k, t):
        half = f // 2
        if 1 <= t < 5:
            return message[main_tile(f, k, t - 1)], message[118 + half * 4 + t - 1], message[126 + half * 4 + t - 1]
        at, corner = y_tile(f, k), 134 if t == 5 else 138
        if k < 3:
            centre = message[at + (t == 0)]
        elif k < 7:
            centre = jnp.where((row < 4) == (t == 5), message[at], 0.0)
        else:
            centre = zero
        return centre, message[corner + half], message[corner + 2 + half]

    def fill(planes, tile_of):
        for plane in planes:
            x = plane % 8
            for h in range(2):
                for field in (fa, fb):
                    field[plane, h, pl.ds(0, 8)] = zero
                    field[plane, h, pl.ds(56, 8)] = zero
            for f in range(3 if 0 < plane < 23 else 1):
                at = (f % 2) * 64 + 8 * x
                for t in range(6):
                    centre, zb, zn = tile_of(f, x, t)
                    side = jnp.where(lane < 8, turn(zn, -at, 1), 0.0)
                    side = jnp.where(lane >= 120, turn(zb, 120 - at, 1), side)
                    if f == 2:
                        if 8 <= plane < 16 and 1 <= t < 5:
                            mass[x, pl.ds(8 * t - 8, 8)] = centre
                        centre, side = inverse(centre), inverse(side)
                    dest, down = ((fa, 8), (src, 0), (inv, 0))[f]
                    dest[plane, 0, pl.ds(8 * t + down, 8)] = centre
                    dest[plane, 1, pl.ds(8 * t + down, 8)] = side

    fill(range(8, 16), own_tile)

    def fill_far(after, before):
        fill(range(8), lambda f, x, t: far_tile(before, f, 7 - x, t))
        fill(range(16, 24), lambda f, x, t: far_tile(after, f, x, t))

    by_parity(px, xa, xb, fill_far)
    xin, xout = fa, fb
    for k, (a, c) in enumerate(factors(SMOOTH_DEG, *SMOOTH)):
        sweep(xin, xout, upd, src, inv, k + 1, 23 - k, a, c, 2, False)
        xin, xout = xout, xin
    def residual(j, row, own_tile, total):
        if 8 <= row < 40:
            tile = pl.ds(row - 8, 8)
            res = (src[8 + j, 0, pl.ds(row, 8)] + total[0]) - (6.0 + mass[j, tile]) * own_tile[0]
            if j % 2 == 0:
                held[row] = res
            else:
                pair[j // 2, tile] = held[row] + res
                pair[4 + j // 2, tile] = mass[j - 1, tile] + mass[j, tile]

    held = {}
    stencil(xin, 8, 8, 2, range(8, 40, 8), residual)
    even = pair[:, pl.ds(0, 16, stride=2), :] + pair[:, pl.ds(1, 16, stride=2), :]
    one = dot(even.reshape(128, 128), coarsen_matrix(lambda r: r // 2)).reshape(2, 4, 16, 128)
    one_out[...] = one
    lane = lanes_like((16, 128))
    for edge, out in ((32, to_next), (0, to_before)):
        for f in range(2):
            packed = jnp.zeros((16, 128), F32)
            for i in range(4):
                packed = jnp.where(lane // 32 == i, turn(one[f, i], 32 * i - edge, 1), packed)
            out[f] = packed


def widen_kernel(one, zbefore, znext, out):
    lane = lanes_like((16, 128))
    for f in range(2):
        for i in range(4):
            v = one[f, i]
            v = jnp.where(lane // 32 == 2, turn(znext[f], 64 - 32 * i, 1), v)
            out[0, f, i] = jnp.where(lane // 32 == 3, turn(zbefore[f], 96 - 32 * i, 1), v)


def rows_kernel(py, near, ya, yb):
    def body(to_next, to_before):
        for start, extra, out in ((8, 7, to_next), (0, 8, to_before)):
            for n in range(32):
                block = near.at[n // 4 % 4, n // 16, n % 4]
                out[n] = block[pl.ds(start, 8)]
                out[32 + n // 8, pl.ds(n % 8, 1)] = block[pl.ds(extra, 1)]

    by_parity(py, ya, yb, body)


def join_kernel(py, near, ya, yb, out):
    row = rows_like((8, 128))

    def body(ynext, ybefore):
        for n in range(32):
            place = n // 4 % 4, n // 16, n % 4
            tile, at = 32 + n // 8, pl.ds(n % 8, 1)
            out[(*place, pl.ds(0, 16))] = near[place]
            out[(*place, pl.ds(16, 8))] = ynext[n]
            mix = jnp.where(row == 0, ynext[tile, at], 0.0)
            out[(*place, pl.ds(24, 8))] = jnp.where(row == 7, ybefore[tile, at], mix)
            out[(*place, pl.ds(32, 8))] = ybefore[n]

    by_parity(py, ya, yb, body)


def middle_kernel(place, py, near, far, fb, src, inv, two_out, ya, yb,
                  fa, upd, mass, pair, pairs):
    zero = jnp.zeros((40, 128), F32)
    for end in (0, 1, 2, 3, 4, 5, 6, 39, 40, 41, 42, 43, 44, 45, 46):
        for field in (fa, fb):
            field[end, 0, pl.ds(8, 40)] = zero
        src[end, 0] = zero
        inv[end, 0] = zero
    (_, scale), *later = factors(SMOOTH_DEG, *SMOOTH)
    for j in range(8):
        group = place[0] ^ ((j & 1) * 4 + (j >> 1 & 1) * 2 + (j >> 2))
        for i in range(4):
            plane = 7 + 4 * group + i
            values = [(near if j < 4 else far)[j % 4, f, i] for f in range(2)]
            mass[plane] = values[1]
            values[1] = inverse(values[1])
            src[plane, 0] = values[0]
            inv[plane, 0] = values[1]
            u = scale * (values[0] * values[1])
            upd[plane, 0] = u
            for t in range(5):
                put(fa, plane, 0, 8 * t, u[8 * t:8 * t + 8], 40, True)
    xin, xout = fa, fb
    for a, c in later:
        sweep(xin, xout, upd, src, inv, 7, 39, a, c, 4, True)
        xin, xout = xout, xin

    def step(n, carry):
        def residual(j, row, own, total):
            p, tile = 7 + 4 * n + j, pl.ds(row, 8)
            res = (src[p, 0, tile] + total[0]) - (6.0 + mass[p, tile]) * own[0]
            if j % 2 == 0:
                held[row] = res
            else:
                pair[2 * n + j // 2, tile] = held[row] + res
                pair[16 + 2 * n + j // 2, tile] = mass[p - 1, tile] + mass[p, tile]

        held = {}
        stencil(xin, 7 + 4 * n, 4, 1, range(0, 40, 8), residual)
        return carry

    lax.fori_loop(0, 8, step, 0)
    even = pair[:, pl.ds(0, 20, stride=2), :] + pair[:, pl.ds(1, 20, stride=2), :]
    pairs[:, pl.ds(0, 20)] = even
    pairs[:, pl.ds(20, 4)] = jnp.zeros((32, 4, 128), F32)
    down = [coarsen_matrix(lambda r, h=h: 64 * h + 16 + jnp.where(r < 96, r // 2, r // 2 - 64)) for h in range(2)]
    for f in range(2):
        low = pairs[pl.ds(16 * f, 8)].reshape(192, 128)
        high = pairs[pl.ds(16 * f + 8, 8)].reshape(192, 128)
        made = (dot(low, down[0]) + dot(high, down[1])).reshape(8, 24, 128)
        def body(to_next, to_before):
            for i in range(8):
                n = 8 * f + i
                at = pl.ds(2 * (n % 4), 2)
                two_out[n] = made[i, 0:8]
                to_next[n] = made[i, 0:8]
                to_before[n] = made[i, 0:8]
                to_next[16 + n // 4, at] = made[i, 18:20]
                to_before[16 + n // 4, at] = made[i, 8:10]

        by_parity(py, ya, yb, body)


def one_hot(shape, axis, source):
    at = lax.broadcasted_iota(jnp.int32, shape, axis)
    return jnp.where(at == source, 1.0, 0.0).astype(F32)


def ascend_kernel(place, py, two, ya, yb, x1, src1, inv1, x0, src0, inv0, out,
                  ca, cb, cupd, csrc, cinv, flat, oa, ob, oupd, za, zb, zupd):
    row = rows_like((8, 128))
    lane = lanes_like((32, 128))
    (_, scale), *later = factors(COARSE_DEG, *COARSE)

    def fill(after, before):
        for i in range(8):
            values = []
            for f in range(2):
                n = 8 * f + i
                mix = jnp.where(row < 2, turn(after[16 + n // 4], -2 * (n % 4), 0), 0.0)
                mix = jnp.where(row >= 6, turn(before[16 + n // 4], 6 - 2 * (n % 4), 0), mix)
                values.append(jnp.concatenate([two[n], after[n], mix, before[n]], axis=0))
            values[1] = inverse(values[1])
            csrc[1 + i, 0] = values[0]
            cinv[1 + i, 0] = values[1]
            u = scale * (values[0] * values[1])
            cupd[1 + i, 0] = u
            for t in range(4):
                put(ca, 1 + i, 0, 8 * t, u[8 * t:8 * t + 8], 32, True)

    by_parity(py, ya, yb, fill)
    xin, xout = ca, cb
    core = pl.ds(8, 32)
    for a, c in later:
        xin[0, 0, core] = jnp.where(lane >= 64, pltpu.roll(xin[8, 0, core], 64, 1), 0.0)
        xin[9, 0, core] = jnp.where(lane < 64, pltpu.roll(xin[1, 0, core], 64, 1), 0.0)
        sweep(xin, xout, cupd, csrc, cinv, 1, 9, a, c, 8, True)
        xin, xout = xout, xin
    zero = jnp.zeros((32, 128), F32)
    for end in (0, 1, 2, 19, 20, 21):
        flat[end] = zero
    for q in range(16):
        v = xin[1 + q % 8, 0, core]
        flat[3 + q] = v if q < 8 else pltpu.roll(v, 64, 1)
    l = lax.broadcasted_iota(jnp.int32, (1, 128), 1)
    wide = one_hot((128, 128), 0, jnp.where(l < 96, 16 + l // 2, l // 2 - 48))
    r = lax.broadcasted_iota(jnp.int32, (40, 1), 0)
    tall = one_hot((40, 32), 1, jnp.where(r < 28, r // 2, 12 + r // 2))
    part = dot(flat[pl.ds(2 * place[0], 8)].reshape(256, 128), wide)
    fine = dot(tall, jnp.concatenate([part[32 * w:32 * w + 32] for w in range(8)], axis=1))
    first = 4 * place[0] + 1
    for w in range(16):
        v = w // 2
        for t in range(5):
            value = x1[first + w, 0, pl.ds(8 + 8 * t, 8)] + fine[8 * t:8 * t + 8, 128 * v:128 * v + 128]
            put(oa, w, 0, 8 * t, value, 40, True)
    xin, xout = oa, ob
    for k, (a, c) in enumerate(factors(SMOOTH_DEG, *SMOOTH)):
        sweep(xin, xout, oupd, src1, inv1, k + 1, 15 - k, a, c, 14 - 2 * k, True, offset=first)
        xin, xout = xout, xin
    side = jnp.where((l < 8) | (l >= 120), 64 + l // 2, -1)
    wide = [one_hot((128, 128), 0, l // 2), one_hot((128, 128), 0, side)]
    r = lax.broadcasted_iota(jnp.int32, (48, 1), 0)
    tall = one_hot((48, 40), 1, jnp.where(r < 8, 36 + r // 2, r // 2 - 4))
    below = xin[4:12, 0, 8:48].reshape(320, 128)
    zero = jnp.zeros((8, 128), F32)
    for h in range(2):
        part = dot(below, wide[h])
        fine = dot(tall, jnp.concatenate([part[40 * w:40 * w + 40] for w in range(8)], axis=1))
        for w in range(16):
            v = w // 2
            za[w, h, pl.ds(8, 48)] = x0[4 + w, h, pl.ds(8, 48)] + fine[:, 128 * v:128 * v + 128]
            for field in (za, zb):
                field[w, h, pl.ds(0, 8)] = zero
                field[w, h, pl.ds(56, 8)] = zero
    xin, xout = za, zb
    for k, (a, c) in enumerate(factors(SMOOTH_DEG, *SMOOTH)):
        sweep(xin, xout, zupd, src0, inv0, k + 1, 15 - k, a, c, 2, False, offset=4)
        xin, xout = xout, xin
    out[...] = xin[4:12, 0, 16:48]


def call(kernel, outs, scratch, *args, spaces=(), limit=24):
    vmem = pl.BlockSpec(memory_space=pltpu.VMEM)
    spaces = [pl.BlockSpec(memory_space=space) for space in spaces]
    scratch = [pltpu.VMEM(s, F32) if isinstance(s, tuple) else s for s in scratch]
    return pl.pallas_call(
        kernel,
        out_shape=[jax.ShapeDtypeStruct(s, F32) for s in outs],
        in_specs=spaces + [vmem] * (len(args) - len(spaces)),
        out_specs=[vmem] * len(outs),
        scratch_shapes=scratch,
        compiler_params=pltpu.CompilerParams(vmem_limit_bytes=limit * 1024 * 1024),
    )(*args)


def shift(value, axis, by):
    count = lax.axis_size(axis)
    pairs = [(i, i + by) for i in range(count) if 0 <= i + by < count]
    return lax.ppermute(value, axis, pairs)


def swap(value, axis, bit):
    return lax.ppermute(value, axis, [(i, i ^ bit) for i in range(lax.axis_size(axis))])


def swap_both(a, b, axis):
    count = lax.axis_size(axis)
    got = []
    for value, first in ((a, 1), (b, 0)):
        ups = [(i, i + 1) for i in range(first, count - 1, 2)]
        got.append(lax.ppermute(value, axis, ups + [(j, i) for i, j in ups]))
    return got


def per_device(right_side, predicted, zone, zone_table):
    px = lax.axis_index("gx").astype(jnp.int32).reshape(1)
    py = lax.axis_index("gy").astype(jnp.int32).reshape(1)
    one_scalar, two_scalars = [pltpu.SMEM], [pltpu.SMEM] * 2
    block = (8, 32, 128)
    main, nxt, bef = call(first_kernel, [(3, *block), (2, 32, 128), (2, 32, 128)],
                          [pltpu.VMEM(block, jnp.int32), pltpu.SemaphoreType.DMA((3,))],
                          zone_table, predicted, right_side, zone,
                          spaces=[pltpu.SMEM, pltpu.HBM, pltpu.HBM, pltpu.HBM], limit=56)
    zbefore, znext = shift(nxt, "gz", 1), shift(bef, "gz", -1)
    ya, yb, main = call(second_kernel, [(28, 8, 128)] * 2 + [(3, *block)], [],
                        py, main, zbefore, znext, spaces=one_scalar)
    ya, yb = swap_both(ya, yb, "gy")
    xa, xb, ybefore, ynext = call(third_kernel, [(TILES, 8, 128)] * 2 + [(28, 8, 128)] * 2, [],
                                  px, py, main, zbefore, znext, ya, yb, spaces=two_scalars)
    xa, xb = swap_both(xa, xb, "gx")
    tall, flat = (24, 2, 64, 128), (24, 2, 48, 128)
    x0, src0, inv0, one, nxt, bef = call(
        descend_kernel,
        [tall, flat, flat, (2, 4, 16, 128), (2, 16, 128), (2, 16, 128)],
        [tall, flat, block, block],
        px, main, zbefore, znext, ybefore, ynext, xa, xb, spaces=one_scalar)
    zbefore, znext = shift(nxt, "gz", 1), shift(bef, "gz", -1)
    near, = call(widen_kernel, [(1, 2, 4, 16, 128)], [], one, zbefore, znext)
    near = jnp.concatenate([near, swap(near, "gx", 4)])
    near = jnp.concatenate([near, swap(near, "gx", 2)])
    ya, yb = call(rows_kernel, [(36, 8, 128)] * 2, [], py, near, spaces=one_scalar)
    ya, yb = swap_both(ya, yb, "gy")
    near, = call(join_kernel, [(4, 2, 4, 40, 128)], [], py, near, ya, yb, spaces=one_scalar)
    far = swap(near, "gx", 1)
    tall, flat = (47, 1, 56, 128), (47, 1, 40, 128)
    x1, src1, inv1, two, ya, yb = call(
        middle_kernel,
        [tall, flat, flat, (16, 8, 128), (20, 8, 128), (20, 8, 128)],
        [tall, flat, (47, 40, 128), (32, 40, 128), (32, 24, 128)],
        px, py, near, far, spaces=two_scalars)
    ya, yb = swap_both(ya, yb, "gy")
    out, = call(
        ascend_kernel,
        [(8, 32, 128)],
        [(10, 1, 48, 128)] * 2 + [(10, 1, 32, 128)] * 3 + [(22, 32, 128)]
        + [(16, 1, 56, 128)] * 2 + [(16, 1, 40, 128)] + [(16, 2, 64, 128)] * 2 + [(16, 2, 48, 128)],
        px, py, two, ya, yb, x1, src1, inv1, x0, src0, inv0, spaces=two_scalars)
    return out


def solution(mesh):
    placed = (P("gx", "gy", "gz"), P("gx", "gy", "gz"), P("gx", "gy", "gz"), P())
    return jax.shard_map(
        per_device, mesh=mesh, in_specs=placed, out_specs=P("gx", "gy", "gz"), check_vma=False
    )
```

```python
import jax
import jax.numpy as jnp
from jax import lax
from jax.experimental import pallas as pl
from jax.experimental.pallas import tpu as pltpu
from jax.sharding import PartitionSpec as P

SMOOTH_DEG = 4
COARSE_DEG = 8
SHIFT = 0.0005
SMOOTH = (0.5, 2.0)
COARSE = (0.1, 2.0)
F32 = jnp.float32
HIGHEST = lax.Precision.HIGHEST


def factors(degree, low, high):
    centre, half = (high + low) / 2.0, (high - low) / 2.0
    ratio = centre / half
    factor = 1.0 / ratio
    pairs = [(0.0, 1.0 / centre)]
    for _ in range(1, degree):
        following = 1.0 / (2.0 * ratio - factor)
        pairs.append((following * factor, 2.0 * following / half))
        factor = following
    return pairs


def lanes_like(shape):
    return lax.broadcasted_iota(jnp.int32, shape, len(shape) - 1)


def rows_like(shape):
    return lax.broadcasted_iota(jnp.int32, shape, len(shape) - 2)


def turn(v, by, axis):
    by = by % v.shape[axis]
    return v if by == 0 else pltpu.roll(v, by, axis)


def across(own, lane):
    up = [turn(v, 1, 1) for v in own]
    down = [turn(v, -1, 1) for v in own]
    if len(own) == 2:
        up = [jnp.where(lane == 0, up[1 - h], up[h]) for h in range(2)]
        down = [jnp.where(lane == 127, down[1 - h], down[h]) for h in range(2)]
    return [p + q for p, q in zip(up, down)]


def put(x, i, h, row, value, height, cyclic):
    x[i, h, pl.ds(8 + row, 8)] = value
    if cyclic and row == 0:
        x[i, h, pl.ds(8 + height, 1)] = value[0:1]
    if cyclic and row == height - 8:
        x[i, h, pl.ds(7, 1)] = value[7:8]


def stencil(x, first, group, halves, rows, use):
    lane = lanes_like((8, 128))
    for row in rows:
        def load(i):
            return [x[i, h, pl.ds(8 + row, 8)] for h in range(halves)]

        below, own = load(first - 1), load(first)
        for j in range(group):
            i = first + j
            above = load(i + 1)
            side = across(own, lane)
            total = [
                (below[h] + above[h]) + (x[i, h, pl.ds(7 + row, 8)] + x[i, h, pl.ds(9 + row, 8)]) + side[h]
                for h in range(halves)
            ]
            use(j, row, own, total)
            below, own = own, above


def sweep(xin, xout, upd, src, inv, start, stop, a, c, group, cyclic, offset=0):
    halves, height = src.shape[1], src.shape[2]

    def body(first):
        def use(j, row, own, total):
            i, tile = first + j, pl.ds(row, 8)
            for h in range(halves):
                g = (src[i + offset, h, tile] + total[h]) * inv[i + offset, h, tile] - own[h]
                u = c * g if a == 0.0 else a * upd[i, h, tile] + c * g
                upd[i, h, tile] = u
                put(xout, i, h, row, own[h] + u, height, cyclic)

        stencil(xin, first, group, halves, range(0, height, 8), use)

    steps = (stop - start) // group
    if steps == 1:
        body(start)
    else:
        def step(n, carry):
            body(start + n * group)
            return carry

        lax.fori_loop(0, steps, step, 0)


def dot(a, b):
    return lax.dot_general(a, b, (((1,), (0,)), ((), ())), precision=HIGHEST, preferred_element_type=F32)


def inverse(mass):
    return jnp.where(mass > 0.0, 1.0 / (6.0 + mass), 0.0)


def by_parity(place, a, b, body):
    odd = place[0] % 2
    pl.when(odd == 1)(lambda: body(a, b))
    pl.when(odd == 0)(lambda: body(b, a))


def first_kernel(table, pred, right, zone, main, to_next, to_before, codes, sems):
    moves = ((zone, codes), (pred, main.at[0]), (right, main.at[1]))
    copies = [pltpu.make_async_copy(*move, sems.at[n]) for n, move in enumerate(moves)]
    for copy in copies:
        copy.start()
    copies[0].wait()
    lane = lanes_like((32, 128))
    for x in range(8):
        code = codes[x]
        absorb = jnp.zeros((32, 128), F32)
        for k in range(16):
            absorb = absorb + jnp.where(code == k, table[k], 0.0)
        main[2, x] = SHIFT + absorb
    copies[1].wait()
    copies[2].wait()
    for edge, out in ((120, to_next), (0, to_before)):
        for half, fields in ((0, (0, 1)), (1, (2,))):
            packed = jnp.zeros((32, 128), F32)
            for n, f in enumerate(fields):
                for x in range(8):
                    at = 64 * n + 8 * x
                    moved = turn(main[f, x], at - edge, 1)
                    packed = jnp.where((lane >= at) & (lane < at + 8), moved, packed)
            out[half] = packed


def second_kernel(py, main, zbefore, znext, ya, yb, kept):
    kept[...] = main[...]

    def body(to_next, to_before):
        for start, out in ((24, to_next), (0, to_before)):
            rows = pl.ds(start, 8)
            for f in range(3):
                for x in range(8):
                    out[f * 8 + x] = main[f, x, rows]
            for half in range(2):
                out[24 + half] = zbefore[half, rows]
                out[26 + half] = znext[half, rows]

    by_parity(py, ya, yb, body)


def main_tile(f, k, t):
    return 4 * k + t + (f > 0) * (32 + 28 * (f - 1))


def y_tile(f, k):
    return 88 + 10 * f + (2 * k if k < 3 else 3 + k)


TILES = 142


def third_kernel(px, py, main, zbefore, znext, ya, yb, xa, xb, ybefore, ynext):
    row = rows_like((8, 128))

    def settle(after, before):
        ynext[...] = after[...]
        ybefore[...] = before[...]

    by_parity(py, ya, yb, settle)

    def body(to_next, to_before):
        for out in (to_next, to_before):
            for k in range(8):
                x = 7 - k if out is to_next else k
                for f in range(3 if k < 7 else 1):
                    for t in range(4):
                        out[main_tile(f, k, t)] = main[f, x, pl.ds(8 * t, 8)]
                    n, at = f * 8 + x, y_tile(f, k)
                    if k < 3:
                        out[at] = ynext[n]
                        out[at + 1] = ybefore[n]
                    elif k < 7:
                        out[at] = jnp.where(row < 4, ynext[n], ybefore[n])
            for half in range(2):
                for t in range(4):
                    out[118 + half * 4 + t] = zbefore[half, pl.ds(8 * t, 8)]
                    out[126 + half * 4 + t] = znext[half, pl.ds(8 * t, 8)]
            out[134:138] = ynext[24:28]
            out[138:142] = ybefore[24:28]

    by_parity(px, xa, xb, body)


def coarsen_matrix(source):
    rows = lax.broadcasted_iota(jnp.int32, (128, 128), 0)
    cols = lax.broadcasted_iota(jnp.int32, (128, 128), 1)
    return jnp.where(source(rows) == cols, 0.5, 0.0).astype(F32)


def descend_kernel(px, main, zbefore, znext, ybefore, ynext, xa, xb, fa, src, inv, one_out, give, keep,
                   fb, upd, mass, pair):
    lane = lanes_like((8, 128))
    row = rows_like((8, 128))
    zero = jnp.zeros((8, 128), F32)

    def own_tile(f, x, t):
        half = f // 2
        if 1 <= t < 5:
            tile = pl.ds(8 * t - 8, 8)
            return main[f, x, tile], zbefore[half, tile], znext[half, tile]
        side = ynext if t == 5 else ybefore
        return side[f * 8 + x], side[24 + half], side[26 + half]

    def far_tile(message, f, k, t):
        half = f // 2
        if 1 <= t < 5:
            return message[main_tile(f, k, t - 1)], message[118 + half * 4 + t - 1], message[126 + half * 4 + t - 1]
        at, corner = y_tile(f, k), 134 if t == 5 else 138
        if k < 3:
            centre = message[at + (t == 0)]
        elif k < 7:
            centre = jnp.where((row < 4) == (t == 5), message[at], 0.0)
        else:
            centre = zero
        return centre, message[corner + half], message[corner + 2 + half]

    def fill(planes, tile_of):
        for plane in planes:
            x = plane % 8
            for h in range(2):
                for field in (fa, fb):
                    field[plane, h, pl.ds(0, 8)] = zero
                    field[plane, h, pl.ds(56, 8)] = zero
            for f in range(3 if 0 < plane < 23 else 1):
                at = (f % 2) * 64 + 8 * x
                for t in range(6):
                    centre, zb, zn = tile_of(f, x, t)
                    side = jnp.where(lane < 8, turn(zn, -at, 1), 0.0)
                    side = jnp.where(lane >= 120, turn(zb, 120 - at, 1), side)
                    if f == 2:
                        if 8 <= plane < 16 and 1 <= t < 5:
                            mass[x, pl.ds(8 * t - 8, 8)] = centre
                        centre, side = inverse(centre), inverse(side)
                    dest, down = ((fa, 8), (src, 0), (inv, 0))[f]
                    dest[plane, 0, pl.ds(8 * t + down, 8)] = centre
                    dest[plane, 1, pl.ds(8 * t + down, 8)] = side

    fill(range(8, 16), own_tile)

    def fill_far(after, before):
        fill(range(8), lambda f, x, t: far_tile(before, f, 7 - x, t))
        fill(range(16, 24), lambda f, x, t: far_tile(after, f, x, t))

    by_parity(px, xa, xb, fill_far)
    xin, xout = fa, fb
    for k, (a, c) in enumerate(factors(SMOOTH_DEG, *SMOOTH)):
        sweep(xin, xout, upd, src, inv, k + 1, 23 - k, a, c, 2, False)
        xin, xout = xout, xin
    def residual(j, row, own_tile, total):
        if 8 <= row < 40:
            tile = pl.ds(row - 8, 8)
            res = (src[8 + j, 0, pl.ds(row, 8)] + total[0]) - (6.0 + mass[j, tile]) * own_tile[0]
            if j % 2 == 0:
                held[row] = res
            else:
                pair[j // 2, tile] = held[row] + res
                pair[4 + j // 2, tile] = mass[j - 1, tile] + mass[j, tile]

    held = {}
    stencil(xin, 8, 8, 2, range(8, 40, 8), residual)
    even = pair[:, pl.ds(0, 16, stride=2), :] + pair[:, pl.ds(1, 16, stride=2), :]
    one = dot(even.reshape(128, 128), coarsen_matrix(lambda r: r // 2)).reshape(2, 4, 16, 128)
    one_out[...] = one
    lane = lanes_like((16, 128))

    def pack(to_next, to_before):
        for edge, out in ((32, to_next), (0, to_before)):
            for f in range(2):
                packed = jnp.zeros((16, 128), F32)
                for i in range(4):
                    packed = jnp.where(lane // 32 == i, turn(one[f, i], 32 * i - edge, 1), packed)
                out[f] = packed

    by_parity(px, give, keep, pack)


def widen_kernel(one, halo, out):
    lane = lanes_like((16, 128))
    for f in range(2):
        for i in range(4):
            v = one[f, i]
            v = jnp.where(lane // 32 == 2, turn(halo[0, f], 64 - 32 * i, 1), v)
            out[0, f, i] = jnp.where(lane // 32 == 3, turn(halo[1, f], 96 - 32 * i, 1), v)


def rows_kernel(py, near, ya, yb):
    def body(to_next, to_before):
        for start, extra, out in ((8, 7, to_next), (0, 8, to_before)):
            for n in range(32):
                block = near.at[n // 4 % 4, n // 16, n % 4]
                out[n] = block[pl.ds(start, 8)]
                out[32 + n // 8, pl.ds(n % 8, 1)] = block[pl.ds(extra, 1)]

    by_parity(py, ya, yb, body)


def join_kernel(py, near, ya, yb, out):
    row = rows_like((8, 128))

    def body(ynext, ybefore):
        for n in range(32):
            place = n // 4 % 4, n // 16, n % 4
            tile, at = 32 + n // 8, pl.ds(n % 8, 1)
            out[(*place, pl.ds(0, 16))] = near[place]
            out[(*place, pl.ds(16, 8))] = ynext[n]
            mix = jnp.where(row == 0, ynext[tile, at], 0.0)
            out[(*place, pl.ds(24, 8))] = jnp.where(row == 7, ybefore[tile, at], mix)
            out[(*place, pl.ds(32, 8))] = ybefore[n]

    by_parity(py, ya, yb, body)


def middle_kernel(place, near, far, fb, src, inv, two_out, edge_out,
                  fa, upd, mass, pair, pairs):
    zero = jnp.zeros((40, 128), F32)
    for end in (0, 1, 2, 3, 4, 5, 6, 39, 40, 41, 42, 43, 44, 45, 46):
        for field in (fa, fb):
            field[end, 0, pl.ds(8, 40)] = zero
        src[end, 0] = zero
        inv[end, 0] = zero
    (_, scale), *later = factors(SMOOTH_DEG, *SMOOTH)
    lane = lanes_like((40, 128))

    def fill(first, second):
        for j in range(4):
            group = (place[0] // 2 * 2) ^ ((j & 1) * 4 + (j >> 1) * 2)
            for i in range(4):
                pairs = []
                for f in range(2):
                    p, q = first[j, f, i], second[j, f, i]
                    v = jnp.where(lane < 96, turn(q, -32, 1), turn(p, 32, 1))
                    pairs.append((jnp.where(lane < 64, p, v), jnp.where(lane < 96, q, p)))
                for core in range(2):
                    plane = 7 + 4 * group + 4 * core + i
                    b1, m1 = pairs[0][core], pairs[1][core]
                    inv1 = inverse(m1)
                    mass[plane] = m1
                    src[plane, 0] = b1
                    inv[plane, 0] = inv1
                    u = scale * (b1 * inv1)
                    upd[plane, 0] = u
                    for t in range(5):
                        put(fa, plane, 0, 8 * t, u[8 * t:8 * t + 8], 40, True)

    by_parity(place, far, near, fill)
    xin, xout = fa, fb
    for a, c in later:
        sweep(xin, xout, upd, src, inv, 7, 39, a, c, 4, True)
        xin, xout = xout, xin

    def step(n, carry):
        def residual(j, row, own, total):
            p, tile = 7 + 4 * n + j, pl.ds(row, 8)
            res = (src[p, 0, tile] + total[0]) - (6.0 + mass[p, tile]) * own[0]
            if j % 2 == 0:
                held[row] = res
            else:
                pair[2 * n + j // 2, tile] = held[row] + res
                pair[16 + 2 * n + j // 2, tile] = mass[p - 1, tile] + mass[p, tile]

        held = {}
        stencil(xin, 7 + 4 * n, 4, 1, range(0, 40, 8), residual)
        return carry

    lax.fori_loop(0, 8, step, 0)
    even = pair[:, pl.ds(0, 20, stride=2), :] + pair[:, pl.ds(1, 20, stride=2), :]
    pairs[:, pl.ds(0, 20)] = even
    pairs[:, pl.ds(20, 4)] = jnp.zeros((32, 4, 128), F32)
    down = [coarsen_matrix(lambda r, h=h: 64 * h + 16 + jnp.where(r < 96, r // 2, r // 2 - 64)) for h in range(2)]
    for f in range(2):
        low = pairs[pl.ds(16 * f, 8)].reshape(192, 128)
        high = pairs[pl.ds(16 * f + 8, 8)].reshape(192, 128)
        made = (dot(low, down[0]) + dot(high, down[1])).reshape(8, 24, 128)
        for i in range(8):
            n = 8 * f + i
            two_out[n] = made[i, 0:8]
            edge_out[n] = made[i, 0:8]
            beyond = jnp.where(place[0] % 2 == 0, made[i, 18:20], made[i, 8:10])
            edge_out[16 + n // 4, pl.ds(2 * (n % 4), 2)] = beyond


def one_hot(shape, axis, source):
    at = lax.broadcasted_iota(jnp.int32, shape, axis)
    return jnp.where(at == source, 1.0, 0.0).astype(F32)


def ascend_kernel(place, two, brought, given, x1, src1, inv1, x0, src0, inv0, out,
                  ca, cb, cupd, csrc, cinv, flat, oa, ob, oupd, za, zb, zupd):
    row = rows_like((8, 128))
    lane = lanes_like((32, 128))
    (_, scale), *later = factors(COARSE_DEG, *COARSE)

    def fill(after, before):
        for i in range(8):
            values = []
            for f in range(2):
                n = 8 * f + i
                mix = jnp.where(row < 2, turn(after[16 + n // 4], -2 * (n % 4), 0), 0.0)
                mix = jnp.where(row >= 6, turn(before[16 + n // 4], 6 - 2 * (n % 4), 0), mix)
                values.append(jnp.concatenate([two[n], after[n], mix, before[n]], axis=0))
            values[1] = inverse(values[1])
            csrc[1 + i, 0] = values[0]
            cinv[1 + i, 0] = values[1]
            u = scale * (values[0] * values[1])
            cupd[1 + i, 0] = u
            for t in range(4):
                put(ca, 1 + i, 0, 8 * t, u[8 * t:8 * t + 8], 32, True)

    by_parity(place, brought, given, fill)
    xin, xout = ca, cb
    core = pl.ds(8, 32)
    for a, c in later:
        xin[0, 0, core] = jnp.where(lane >= 64, pltpu.roll(xin[8, 0, core], 64, 1), 0.0)
        xin[9, 0, core] = jnp.where(lane < 64, pltpu.roll(xin[1, 0, core], 64, 1), 0.0)
        sweep(xin, xout, cupd, csrc, cinv, 1, 9, a, c, 8, True)
        xin, xout = xout, xin
    zero = jnp.zeros((32, 128), F32)
    for end in (0, 1, 2, 19, 20, 21):
        flat[end] = zero
    for q in range(16):
        v = xin[1 + q % 8, 0, core]
        flat[3 + q] = v if q < 8 else pltpu.roll(v, 64, 1)
    l = lax.broadcasted_iota(jnp.int32, (1, 128), 1)
    wide = one_hot((128, 128), 0, jnp.where(l < 96, 16 + l // 2, l // 2 - 48))
    r = lax.broadcasted_iota(jnp.int32, (40, 1), 0)
    tall = one_hot((40, 32), 1, jnp.where(r < 28, r // 2, 12 + r // 2))
    part = dot(flat[pl.ds(2 * place[0], 8)].reshape(256, 128), wide)
    fine = dot(tall, jnp.concatenate([part[32 * w:32 * w + 32] for w in range(8)], axis=1))
    first = 4 * place[0] + 1
    for w in range(16):
        v = w // 2
        for t in range(5):
            value = x1[first + w, 0, pl.ds(8 + 8 * t, 8)] + fine[8 * t:8 * t + 8, 128 * v:128 * v + 128]
            put(oa, w, 0, 8 * t, value, 40, True)
    xin, xout = oa, ob
    for k, (a, c) in enumerate(factors(SMOOTH_DEG, *SMOOTH)):
        sweep(xin, xout, oupd, src1, inv1, k + 1, 15 - k, a, c, 14 - 2 * k, True, offset=first)
        xin, xout = xout, xin
    side = jnp.where((l < 8) | (l >= 120), 64 + l // 2, -1)
    wide = [one_hot((128, 128), 0, l // 2), one_hot((128, 128), 0, side)]
    r = lax.broadcasted_iota(jnp.int32, (48, 1), 0)
    tall = one_hot((48, 40), 1, jnp.where(r < 8, 36 + r // 2, r // 2 - 4))
    below = xin[4:12, 0, 8:48].reshape(320, 128)
    zero = jnp.zeros((8, 128), F32)
    for h in range(2):
        part = dot(below, wide[h])
        fine = dot(tall, jnp.concatenate([part[40 * w:40 * w + 40] for w in range(8)], axis=1))
        for w in range(16):
            v = w // 2
            za[w, h, pl.ds(8, 48)] = x0[4 + w, h, pl.ds(8, 48)] + fine[:, 128 * v:128 * v + 128]
            for field in (za, zb):
                field[w, h, pl.ds(0, 8)] = zero
                field[w, h, pl.ds(56, 8)] = zero
    xin, xout = za, zb
    for k, (a, c) in enumerate(factors(SMOOTH_DEG, *SMOOTH)):
        sweep(xin, xout, zupd, src0, inv0, k + 1, 15 - k, a, c, 2, False, offset=4)
        xin, xout = xout, xin
    out[...] = xin[4:12, 0, 16:48]


def call(kernel, outs, scratch, *args, spaces=(), limit=24):
    vmem = pl.BlockSpec(memory_space=pltpu.VMEM)
    spaces = [pl.BlockSpec(memory_space=space) for space in spaces]
    scratch = [pltpu.VMEM(s, F32) if isinstance(s, tuple) else s for s in scratch]
    return pl.pallas_call(
        kernel,
        out_shape=[jax.ShapeDtypeStruct(s, F32) for s in outs],
        in_specs=spaces + [vmem] * (len(args) - len(spaces)),
        out_specs=[vmem] * len(outs),
        scratch_shapes=scratch,
        compiler_params=pltpu.CompilerParams(vmem_limit_bytes=limit * 1024 * 1024),
    )(*args)


def shift(value, axis, by):
    count = lax.axis_size(axis)
    pairs = [(i, i + by) for i in range(count) if 0 <= i + by < count]
    return lax.ppermute(value, axis, pairs)


def swap(value, axis, bit):
    return lax.ppermute(value, axis, [(i, i ^ bit) for i in range(lax.axis_size(axis))])


def swap_both(a, b, axis):
    count = lax.axis_size(axis)
    got = []
    for value, first in ((a, 1), (b, 0)):
        ups = [(i, i + 1) for i in range(first, count - 1, 2)]
        got.append(lax.ppermute(value, axis, ups + [(j, i) for i, j in ups]))
    return got


def cross(value, axis):
    count = lax.axis_size(axis)
    pairs = []
    for g in range(lax.axis_size("gx")):
        by = 1 - 2 * (g % 2)
        pairs += [(g * count + i, g * count + i + by) for i in range(count) if 0 <= i + by < count]
    return lax.ppermute(value, ("gx", axis), pairs)


def per_device(right_side, predicted, zone, zone_table):
    px = lax.axis_index("gx").astype(jnp.int32).reshape(1)
    py = lax.axis_index("gy").astype(jnp.int32).reshape(1)
    one_scalar, two_scalars = [pltpu.SMEM], [pltpu.SMEM] * 2
    block = (8, 32, 128)
    main, nxt, bef = call(first_kernel, [(3, *block), (2, 32, 128), (2, 32, 128)],
                          [pltpu.VMEM(block, jnp.int32), pltpu.SemaphoreType.DMA((3,))],
                          zone_table, predicted, right_side, zone,
                          spaces=[pltpu.SMEM, pltpu.HBM, pltpu.HBM, pltpu.HBM], limit=56)
    zbefore, znext = shift(nxt, "gz", 1), shift(bef, "gz", -1)
    ya, yb, main = call(second_kernel, [(28, 8, 128)] * 2 + [(3, *block)], [],
                        py, main, zbefore, znext, spaces=one_scalar)
    ya, yb = swap_both(ya, yb, "gy")
    xa, xb, ybefore, ynext = call(third_kernel, [(TILES, 8, 128)] * 2 + [(28, 8, 128)] * 2, [],
                                  px, py, main, zbefore, znext, ya, yb, spaces=two_scalars)
    xa, xb = swap_both(xa, xb, "gx")
    tall, flat = (24, 2, 64, 128), (24, 2, 48, 128)
    x0, src0, inv0, one, give, keep = call(
        descend_kernel,
        [tall, flat, flat, (2, 4, 16, 128), (2, 16, 128), (2, 16, 128)],
        [tall, flat, block, block],
        px, main, zbefore, znext, ybefore, ynext, xa, xb, spaces=one_scalar)
    halo = cross(jnp.stack([keep, swap(give, "gx", 1)]), "gz")
    near, = call(widen_kernel, [(1, 2, 4, 16, 128)], [], one, halo)
    near = jnp.concatenate([near, swap(near, "gx", 4)])
    near = jnp.concatenate([near, swap(near, "gx", 2)])
    ya, yb = call(rows_kernel, [(36, 8, 128)] * 2, [], py, near, spaces=one_scalar)
    ya, yb = swap_both(ya, yb, "gy")
    near, = call(join_kernel, [(4, 2, 4, 40, 128)], [], py, near, ya, yb, spaces=one_scalar)
    far = swap(near, "gx", 1)
    tall, flat = (47, 1, 56, 128), (47, 1, 40, 128)
    x1, src1, inv1, two, edge = call(
        middle_kernel,
        [tall, flat, flat, (16, 8, 128), (20, 8, 128)],
        [tall, flat, (47, 40, 128), (32, 40, 128), (32, 24, 128)],
        px, near, far, spaces=one_scalar)
    brought = cross(edge, "gy")
    given = swap(brought, "gx", 1)
    out, = call(
        ascend_kernel,
        [(8, 32, 128)],
        [(10, 1, 48, 128)] * 2 + [(10, 1, 32, 128)] * 3 + [(22, 32, 128)]
        + [(16, 1, 56, 128)] * 2 + [(16, 1, 40, 128)] + [(16, 2, 64, 128)] * 2 + [(16, 2, 48, 128)],
        px, two, brought, given, x1, src1, inv1, x0, src0, inv0, spaces=one_scalar)
    return out


def solution(mesh):
    placed = (P("gx", "gy", "gz"), P("gx", "gy", "gz"), P("gx", "gy", "gz"), P())
    return jax.shard_map(
        per_device, mesh=mesh, in_specs=placed, out_specs=P("gx", "gy", "gz"), check_vma=False
    )
```

```python
import jax
import jax.numpy as jnp
from jax import lax
from jax.experimental import pallas as pl
from jax.experimental.pallas import tpu as pltpu
from jax.sharding import PartitionSpec as P

SMOOTH_DEG = 4
COARSE_DEG = 8
SHIFT = 0.0005
SMOOTH = (0.5, 2.0)
COARSE = (0.1, 2.0)
F32 = jnp.float32
HIGHEST = lax.Precision.HIGHEST


def factors(degree, low, high):
    centre, half = (high + low) / 2.0, (high - low) / 2.0
    ratio = centre / half
    factor = 1.0 / ratio
    pairs = [(0.0, 1.0 / centre)]
    for _ in range(1, degree):
        following = 1.0 / (2.0 * ratio - factor)
        pairs.append((following * factor, 2.0 * following / half))
        factor = following
    return pairs


def lanes_like(shape):
    return lax.broadcasted_iota(jnp.int32, shape, len(shape) - 1)


def rows_like(shape):
    return lax.broadcasted_iota(jnp.int32, shape, len(shape) - 2)


def turn(v, by, axis):
    by = by % v.shape[axis]
    return v if by == 0 else pltpu.roll(v, by, axis)


def across(own, lane):
    up = [turn(v, 1, 1) for v in own]
    down = [turn(v, -1, 1) for v in own]
    if len(own) == 2:
        up = [jnp.where(lane == 0, up[1 - h], up[h]) for h in range(2)]
        down = [jnp.where(lane == 127, down[1 - h], down[h]) for h in range(2)]
    return [p + q for p, q in zip(up, down)]


def put(x, i, h, row, value, height, cyclic):
    x[i, h, pl.ds(8 + row, 8)] = value
    if cyclic and row == 0:
        x[i, h, pl.ds(8 + height, 1)] = value[0:1]
    if cyclic and row == height - 8:
        x[i, h, pl.ds(7, 1)] = value[7:8]


def stencil(x, first, group, halves, rows, use, flush=None):
    lane = lanes_like((8, 128))
    for row in rows:
        def load(i):
            return [x[i, h, pl.ds(8 + row, 8)] for h in range(halves)]

        below, own = load(first - 1), load(first)
        for j in range(group):
            i = first + j
            above = load(i + 1)
            side = across(own, lane)
            total = [
                (below[h] + above[h]) + (x[i, h, pl.ds(7 + row, 8)] + x[i, h, pl.ds(9 + row, 8)]) + side[h]
                for h in range(halves)
            ]
            use(j, row, own, total)
            below, own = own, above
        if flush is not None and (group > 4 or row // 8 % 2 == 1 or row == rows[-1]):
            flush()


def sweep(xin, xout, upd, src, inv, start, stop, a, c, group, cyclic, offset=0):
    halves, height = src.shape[1], src.shape[2]

    def body(first):
        def use(j, row, own, total):
            i, tile = first + j, pl.ds(row, 8)
            for h in range(halves):
                g = (src[i + offset, h, tile] + total[h]) * inv[i + offset, h, tile] - own[h]
                u = c * g if a == 0.0 else a * upd[i, h, tile] + c * g
                made.append((i, h, row, u, own[h] + u))

        def flush():
            for i, h, row, u, value in made:
                upd[i, h, pl.ds(row, 8)] = u
                put(xout, i, h, row, value, height, cyclic)
            made.clear()

        made = []
        stencil(xin, first, group, halves, range(0, height, 8), use, flush)

    steps = (stop - start) // group
    if steps == 1:
        body(start)
    else:
        def step(n, carry):
            body(start + n * group)
            return carry

        lax.fori_loop(0, steps, step, 0)


def dot(a, b):
    return lax.dot_general(a, b, (((1,), (0,)), ((), ())), precision=HIGHEST, preferred_element_type=F32)


def inverse(mass):
    return jnp.where(mass > 0.0, 1.0 / (6.0 + mass), 0.0)


def by_parity(place, a, b, body):
    odd = place[0] % 2
    pl.when(odd == 1)(lambda: body(a, b))
    pl.when(odd == 0)(lambda: body(b, a))


def first_kernel(table, pred, right, zone, main, to_next, to_before, codes, sems):
    moves = ((zone, codes), (pred, main.at[0]), (right, main.at[1]))
    copies = [pltpu.make_async_copy(*move, sems.at[n]) for n, move in enumerate(moves)]
    for copy in copies:
        copy.start()
    copies[0].wait()
    lane = lanes_like((32, 128))
    for x in range(8):
        code = codes[x]
        absorb = jnp.zeros((32, 128), F32)
        for k in range(16):
            absorb = absorb + jnp.where(code == k, table[k], 0.0)
        main[2, x] = SHIFT + absorb
    copies[1].wait()
    copies[2].wait()
    for edge, out in ((120, to_next), (0, to_before)):
        for half, fields in ((0, (0, 1)), (1, (2,))):
            packed = jnp.zeros((32, 128), F32)
            for n, f in enumerate(fields):
                for x in range(8):
                    at = 64 * n + 8 * x
                    moved = turn(main[f, x], at - edge, 1)
                    packed = jnp.where((lane >= at) & (lane < at + 8), moved, packed)
            out[half] = packed


def second_kernel(py, main, zbefore, znext, ya, yb, kept):
    kept[...] = main[...]

    def body(to_next, to_before):
        for start, out in ((24, to_next), (0, to_before)):
            rows = pl.ds(start, 8)
            for f in range(3):
                for x in range(8):
                    out[f * 8 + x] = main[f, x, rows]
            for half in range(2):
                out[24 + half] = zbefore[half, rows]
                out[26 + half] = znext[half, rows]

    by_parity(py, ya, yb, body)


def main_tile(f, k, t):
    return 4 * k + t + (f > 0) * (32 + 28 * (f - 1))


def y_tile(f, k):
    return 88 + 10 * f + (2 * k if k < 3 else 3 + k)


TILES = 142


def third_kernel(px, py, main, zbefore, znext, ya, yb, xa, xb, ybefore, ynext):
    row = rows_like((8, 128))

    def settle(after, before):
        ynext[...] = after[...]
        ybefore[...] = before[...]

    by_parity(py, ya, yb, settle)

    def body(to_next, to_before):
        for out in (to_next, to_before):
            for k in range(8):
                x = 7 - k if out is to_next else k
                for f in range(3 if k < 7 else 1):
                    for t in range(4):
                        out[main_tile(f, k, t)] = main[f, x, pl.ds(8 * t, 8)]
                    n, at = f * 8 + x, y_tile(f, k)
                    if k < 3:
                        out[at] = ynext[n]
                        out[at + 1] = ybefore[n]
                    elif k < 7:
                        out[at] = jnp.where(row < 4, ynext[n], ybefore[n])
            for half in range(2):
                for t in range(4):
                    out[118 + half * 4 + t] = zbefore[half, pl.ds(8 * t, 8)]
                    out[126 + half * 4 + t] = znext[half, pl.ds(8 * t, 8)]
            out[134:138] = ynext[24:28]
            out[138:142] = ybefore[24:28]

    by_parity(px, xa, xb, body)


def coarsen_matrix(source):
    rows = lax.broadcasted_iota(jnp.int32, (128, 128), 0)
    cols = lax.broadcasted_iota(jnp.int32, (128, 128), 1)
    return jnp.where(source(rows) == cols, 0.5, 0.0).astype(F32)


def descend_kernel(px, main, zbefore, znext, ybefore, ynext, xa, xb, fa, src, inv, one_out, give, keep,
                   fb, upd, mass, pair):
    lane = lanes_like((8, 128))
    row = rows_like((8, 128))
    zero = jnp.zeros((8, 128), F32)

    def own_tile(f, x, t):
        half = f // 2
        if 1 <= t < 5:
            tile = pl.ds(8 * t - 8, 8)
            return main[f, x, tile], zbefore[half, tile], znext[half, tile]
        side = ynext if t == 5 else ybefore
        return side[f * 8 + x], side[24 + half], side[26 + half]

    def far_tile(message, f, k, t):
        half = f // 2
        if 1 <= t < 5:
            return message[main_tile(f, k, t - 1)], message[118 + half * 4 + t - 1], message[126 + half * 4 + t - 1]
        at, corner = y_tile(f, k), 134 if t == 5 else 138
        if k < 3:
            centre = message[at + (t == 0)]
        elif k < 7:
            centre = jnp.where((row < 4) == (t == 5), message[at], 0.0)
        else:
            centre = zero
        return centre, message[corner + half], message[corner + 2 + half]

    def fill(planes, tile_of):
        for plane in planes:
            x = plane % 8
            for h in range(2):
                for field in (fa, fb):
                    field[plane, h, pl.ds(0, 8)] = zero
                    field[plane, h, pl.ds(56, 8)] = zero
            for f in range(3 if 0 < plane < 23 else 1):
                at = (f % 2) * 64 + 8 * x
                for t in range(6):
                    centre, zb, zn = tile_of(f, x, t)
                    side = jnp.where(lane < 8, turn(zn, -at, 1), 0.0)
                    side = jnp.where(lane >= 120, turn(zb, 120 - at, 1), side)
                    if f == 2:
                        if 8 <= plane < 16 and 1 <= t < 5:
                            mass[x, pl.ds(8 * t - 8, 8)] = centre
                        centre, side = inverse(centre), inverse(side)
                    dest, down = ((fa, 8), (src, 0), (inv, 0))[f]
                    dest[plane, 0, pl.ds(8 * t + down, 8)] = centre
                    dest[plane, 1, pl.ds(8 * t + down, 8)] = side

    fill(range(8, 16), own_tile)

    def fill_far(after, before):
        fill(range(8), lambda f, x, t: far_tile(before, f, 7 - x, t))
        fill(range(16, 24), lambda f, x, t: far_tile(after, f, x, t))

    by_parity(px, xa, xb, fill_far)
    xin, xout = fa, fb
    for k, (a, c) in enumerate(factors(SMOOTH_DEG, *SMOOTH)):
        sweep(xin, xout, upd, src, inv, k + 1, 23 - k, a, c, 2, False)
        xin, xout = xout, xin
    def residual(j, row, own_tile, total):
        if 8 <= row < 40:
            tile = pl.ds(row - 8, 8)
            res = (src[8 + j, 0, pl.ds(row, 8)] + total[0]) - (6.0 + mass[j, tile]) * own_tile[0]
            if j % 2 == 0:
                held[row] = res
            else:
                pair[j // 2, tile] = held[row] + res
                pair[4 + j // 2, tile] = mass[j - 1, tile] + mass[j, tile]

    held = {}
    stencil(xin, 8, 8, 2, range(8, 40, 8), residual)
    even = pair[:, pl.ds(0, 16, stride=2), :] + pair[:, pl.ds(1, 16, stride=2), :]
    one = dot(even.reshape(128, 128), coarsen_matrix(lambda r: r // 2)).reshape(2, 4, 16, 128)
    one_out[...] = one
    lane = lanes_like((16, 128))

    def pack(to_next, to_before):
        for edge, out in ((32, to_next), (0, to_before)):
            for f in range(2):
                packed = jnp.zeros((16, 128), F32)
                for i in range(4):
                    packed = jnp.where(lane // 32 == i, turn(one[f, i], 32 * i - edge, 1), packed)
                out[f] = packed

    by_parity(px, give, keep, pack)


def widen_kernel(one, halo, out):
    lane = lanes_like((16, 128))
    for f in range(2):
        for i in range(4):
            v = one[f, i]
            v = jnp.where(lane // 32 == 2, turn(halo[0, f], 64 - 32 * i, 1), v)
            out[0, f, i] = jnp.where(lane // 32 == 3, turn(halo[1, f], 96 - 32 * i, 1), v)


def rows_kernel(py, near, ya, yb):
    def body(to_next, to_before):
        for start, extra, out in ((8, 7, to_next), (0, 8, to_before)):
            for n in range(32):
                block = near.at[n // 4 % 4, n // 16, n % 4]
                out[n] = block[pl.ds(start, 8)]
                out[32 + n // 8, pl.ds(n % 8, 1)] = block[pl.ds(extra, 1)]

    by_parity(py, ya, yb, body)


def join_kernel(py, near, ya, yb, out):
    row = rows_like((8, 128))

    def body(ynext, ybefore):
        for n in range(32):
            place = n // 4 % 4, n // 16, n % 4
            tile, at = 32 + n // 8, pl.ds(n % 8, 1)
            out[(*place, pl.ds(0, 16))] = near[place]
            out[(*place, pl.ds(16, 8))] = ynext[n]
            mix = jnp.where(row == 0, ynext[tile, at], 0.0)
            out[(*place, pl.ds(24, 8))] = jnp.where(row == 7, ybefore[tile, at], mix)
            out[(*place, pl.ds(32, 8))] = ybefore[n]

    by_parity(py, ya, yb, body)


def middle_kernel(place, near, far, fb, src, inv, two_out, edge_out,
                  fa, upd, mass, pair, pairs):
    zero = jnp.zeros((40, 128), F32)
    for end in (0, 1, 2, 3, 4, 5, 6, 39, 40, 41, 42, 43, 44, 45, 46):
        for field in (fa, fb):
            field[end, 0, pl.ds(8, 40)] = zero
        src[end, 0] = zero
        inv[end, 0] = zero
    (_, scale), *later = factors(SMOOTH_DEG, *SMOOTH)
    lane = lanes_like((40, 128))

    def fill(first, second):
        for j in range(4):
            group = (place[0] // 2 * 2) ^ ((j & 1) * 4 + (j >> 1) * 2)
            for i in range(4):
                pairs = []
                for f in range(2):
                    p, q = first[j, f, i], second[j, f, i]
                    v = jnp.where(lane < 96, turn(q, -32, 1), turn(p, 32, 1))
                    pairs.append((jnp.where(lane < 64, p, v), jnp.where(lane < 96, q, p)))
                for core in range(2):
                    plane = 7 + 4 * group + 4 * core + i
                    b1, m1 = pairs[0][core], pairs[1][core]
                    inv1 = inverse(m1)
                    mass[plane] = m1
                    src[plane, 0] = b1
                    inv[plane, 0] = inv1
                    u = scale * (b1 * inv1)
                    upd[plane, 0] = u
                    for t in range(5):
                        put(fa, plane, 0, 8 * t, u[8 * t:8 * t + 8], 40, True)

    by_parity(place, far, near, fill)
    xin, xout = fa, fb
    for a, c in later:
        sweep(xin, xout, upd, src, inv, 7, 39, a, c, 4, True)
        xin, xout = xout, xin

    def step(n, carry):
        def residual(j, row, own, total):
            p, tile = 7 + 4 * n + j, pl.ds(row, 8)
            res = (src[p, 0, tile] + total[0]) - (6.0 + mass[p, tile]) * own[0]
            if j % 2 == 0:
                held[row] = res
            else:
                pair[2 * n + j // 2, tile] = held[row] + res
                pair[16 + 2 * n + j // 2, tile] = mass[p - 1, tile] + mass[p, tile]

        held = {}
        stencil(xin, 7 + 4 * n, 4, 1, range(0, 40, 8), residual)
        return carry

    lax.fori_loop(0, 8, step, 0)
    even = pair[:, pl.ds(0, 20, stride=2), :] + pair[:, pl.ds(1, 20, stride=2), :]
    pairs[:, pl.ds(0, 20)] = even
    pairs[:, pl.ds(20, 4)] = jnp.zeros((32, 4, 128), F32)
    down = [coarsen_matrix(lambda r, h=h: 64 * h + 16 + jnp.where(r < 96, r // 2, r // 2 - 64)) for h in range(2)]
    for f in range(2):
        low = pairs[pl.ds(16 * f, 8)].reshape(192, 128)
        high = pairs[pl.ds(16 * f + 8, 8)].reshape(192, 128)
        made = (dot(low, down[0]) + dot(high, down[1])).reshape(8, 24, 128)
        for i in range(8):
            n = 8 * f + i
            two_out[n] = made[i, 0:8]
            edge_out[n] = made[i, 0:8]
            beyond = jnp.where(place[0] % 2 == 0, made[i, 18:20], made[i, 8:10])
            edge_out[16 + n // 4, pl.ds(2 * (n % 4), 2)] = beyond


def double(x, i, h, row, value):
    for odd in range(2):
        x.at[i, h][pl.ds(row + odd, value.shape[0], stride=2), :] = value


def one_hot(shape, axis, source):
    at = lax.broadcasted_iota(jnp.int32, shape, axis)
    return jnp.where(at == source, 1.0, 0.0).astype(F32)


def ascend_kernel(place, two, brought, given, x1, src1, inv1, x0, src0, inv0, out,
                  ca, cb, cupd, csrc, cinv, flat, oa, ob, oupd, za, zb, zupd):
    row = rows_like((8, 128))
    lane = lanes_like((32, 128))
    (_, scale), *later = factors(COARSE_DEG, *COARSE)

    def fill(after, before):
        for i in range(8):
            values = []
            for f in range(2):
                n = 8 * f + i
                mix = jnp.where(row < 2, turn(after[16 + n // 4], -2 * (n % 4), 0), 0.0)
                mix = jnp.where(row >= 6, turn(before[16 + n // 4], 6 - 2 * (n % 4), 0), mix)
                values.append(jnp.concatenate([two[n], after[n], mix, before[n]], axis=0))
            values[1] = inverse(values[1])
            csrc[1 + i, 0] = values[0]
            cinv[1 + i, 0] = values[1]
            u = scale * (values[0] * values[1])
            cupd[1 + i, 0] = u
            for t in range(4):
                put(ca, 1 + i, 0, 8 * t, u[8 * t:8 * t + 8], 32, True)

    by_parity(place, brought, given, fill)
    xin, xout = ca, cb
    core = pl.ds(8, 32)
    for a, c in later:
        xin[0, 0, core] = jnp.where(lane >= 64, pltpu.roll(xin[8, 0, core], 64, 1), 0.0)
        xin[9, 0, core] = jnp.where(lane < 64, pltpu.roll(xin[1, 0, core], 64, 1), 0.0)
        sweep(xin, xout, cupd, csrc, cinv, 1, 9, a, c, 8, True)
        xin, xout = xout, xin
    zero = jnp.zeros((32, 128), F32)
    for end in (0, 1, 2, 19, 20, 21):
        flat[end] = zero
    for q in range(16):
        v = xin[1 + q % 8, 0, core]
        flat[3 + q] = v if q < 8 else pltpu.roll(v, 64, 1)
    l = lax.broadcasted_iota(jnp.int32, (1, 128), 1)
    wide = one_hot((128, 128), 0, jnp.where(l < 96, 16 + l // 2, l // 2 - 48))
    part = dot(flat[pl.ds(2 * place[0], 8)].reshape(256, 128), wide)
    first = 4 * place[0] + 1
    for v in range(8):
        double(oa, 2 * v, 0, 32, part[32 * v + 24:32 * v + 32])
        double(oa, 2 * v, 0, 8, part[32 * v:32 * v + 14])
        for t in range(5):
            fine = oa[2 * v, 0, pl.ds(8 + 8 * t, 8)]
            for w in (2 * v, 2 * v + 1):
                put(oa, w, 0, 8 * t, x1[first + w, 0, pl.ds(8 + 8 * t, 8)] + fine, 40, True)
    xin, xout = oa, ob
    for k, (a, c) in enumerate(factors(SMOOTH_DEG, *SMOOTH)):
        sweep(xin, xout, oupd, src1, inv1, k + 1, 15 - k, a, c, 14 - 2 * k, True, offset=first)
        xin, xout = xout, xin
    side = jnp.where((l < 8) | (l >= 120), 64 + l // 2, -1)
    wide = [one_hot((128, 128), 0, l // 2), one_hot((128, 128), 0, side)]
    below = xin[4:12, 0, 8:48].reshape(320, 128)
    zero = jnp.zeros((8, 128), F32)
    for h in range(2):
        part = dot(below, wide[h])
        for v in range(8):
            double(za, 2 * v, h, 0, part[40 * v + 32:40 * v + 40])
            double(za, 2 * v, h, 16, part[40 * v:40 * v + 20])
            for t in range(6):
                tile = pl.ds(8 + 8 * t, 8)
                fine = za[2 * v, h, tile]
                for w in (2 * v, 2 * v + 1):
                    za[w, h, tile] = x0[4 + w, h, tile] + fine
            for w in (2 * v, 2 * v + 1):
                for field in (za, zb):
                    field[w, h, pl.ds(0, 8)] = zero
                    field[w, h, pl.ds(56, 8)] = zero
    xin, xout = za, zb
    for k, (a, c) in enumerate(factors(SMOOTH_DEG, *SMOOTH)):
        sweep(xin, xout, zupd, src0, inv0, k + 1, 15 - k, a, c, 2, False, offset=4)
        xin, xout = xout, xin
    out[...] = xin[4:12, 0, 16:48]


def call(kernel, outs, scratch, *args, spaces=(), limit=24):
    vmem = pl.BlockSpec(memory_space=pltpu.VMEM)
    spaces = [pl.BlockSpec(memory_space=space) for space in spaces]
    scratch = [pltpu.VMEM(s, F32) if isinstance(s, tuple) else s for s in scratch]
    return pl.pallas_call(
        kernel,
        out_shape=[jax.ShapeDtypeStruct(s, F32) for s in outs],
        in_specs=spaces + [vmem] * (len(args) - len(spaces)),
        out_specs=[vmem] * len(outs),
        scratch_shapes=scratch,
        compiler_params=pltpu.CompilerParams(vmem_limit_bytes=limit * 1024 * 1024),
    )(*args)


def shift(value, axis, by):
    count = lax.axis_size(axis)
    pairs = [(i, i + by) for i in range(count) if 0 <= i + by < count]
    return lax.ppermute(value, axis, pairs)


def swap(value, axis, bit):
    return lax.ppermute(value, axis, [(i, i ^ bit) for i in range(lax.axis_size(axis))])


def swap_both(a, b, axis):
    count = lax.axis_size(axis)
    got = []
    for value, first in ((a, 1), (b, 0)):
        ups = [(i, i + 1) for i in range(first, count - 1, 2)]
        got.append(lax.ppermute(value, axis, ups + [(j, i) for i, j in ups]))
    return got


def cross(value, axis):
    count = lax.axis_size(axis)
    pairs = []
    for g in range(lax.axis_size("gx")):
        by = 1 - 2 * (g % 2)
        pairs += [(g * count + i, g * count + i + by) for i in range(count) if 0 <= i + by < count]
    return lax.ppermute(value, ("gx", axis), pairs)


def per_device(right_side, predicted, zone, zone_table):
    px = lax.axis_index("gx").astype(jnp.int32).reshape(1)
    py = lax.axis_index("gy").astype(jnp.int32).reshape(1)
    one_scalar, two_scalars = [pltpu.SMEM], [pltpu.SMEM] * 2
    block = (8, 32, 128)
    main, nxt, bef = call(first_kernel, [(3, *block), (2, 32, 128), (2, 32, 128)],
                          [pltpu.VMEM(block, jnp.int32), pltpu.SemaphoreType.DMA((3,))],
                          zone_table, predicted, right_side, zone,
                          spaces=[pltpu.SMEM, pltpu.HBM, pltpu.HBM, pltpu.HBM], limit=56)
    zbefore, znext = shift(nxt, "gz", 1), shift(bef, "gz", -1)
    ya, yb, main = call(second_kernel, [(28, 8, 128)] * 2 + [(3, *block)], [],
                        py, main, zbefore, znext, spaces=one_scalar)
    ya, yb = swap_both(ya, yb, "gy")
    xa, xb, ybefore, ynext = call(third_kernel, [(TILES, 8, 128)] * 2 + [(28, 8, 128)] * 2, [],
                                  px, py, main, zbefore, znext, ya, yb, spaces=two_scalars)
    xa, xb = swap_both(xa, xb, "gx")
    tall, flat = (24, 2, 64, 128), (24, 2, 48, 128)
    x0, src0, inv0, one, give, keep = call(
        descend_kernel,
        [tall, flat, flat, (2, 4, 16, 128), (2, 16, 128), (2, 16, 128)],
        [tall, flat, block, block],
        px, main, zbefore, znext, ybefore, ynext, xa, xb, spaces=one_scalar)
    halo = cross(jnp.stack([keep, swap(give, "gx", 1)]), "gz")
    near, = call(widen_kernel, [(1, 2, 4, 16, 128)], [], one, halo)
    near = jnp.concatenate([near, swap(near, "gx", 4)])
    near = jnp.concatenate([near, swap(near, "gx", 2)])
    ya, yb = call(rows_kernel, [(36, 8, 128)] * 2, [], py, near, spaces=one_scalar)
    ya, yb = swap_both(ya, yb, "gy")
    near, = call(join_kernel, [(4, 2, 4, 40, 128)], [], py, near, ya, yb, spaces=one_scalar)
    far = swap(near, "gx", 1)
    tall, flat = (47, 1, 56, 128), (47, 1, 40, 128)
    x1, src1, inv1, two, edge = call(
        middle_kernel,
        [tall, flat, flat, (16, 8, 128), (20, 8, 128)],
        [tall, flat, (47, 40, 128), (32, 40, 128), (32, 24, 128)],
        px, near, far, spaces=one_scalar)
    brought = cross(edge, "gy")
    given = swap(brought, "gx", 1)
    out, = call(
        ascend_kernel,
        [(8, 32, 128)],
        [(10, 1, 48, 128)] * 2 + [(10, 1, 32, 128)] * 3 + [(22, 32, 128)]
        + [(16, 1, 56, 128)] * 2 + [(16, 1, 40, 128)] + [(16, 2, 64, 128)] * 2 + [(16, 2, 48, 128)],
        px, two, brought, given, x1, src1, inv1, x0, src0, inv0, spaces=one_scalar)
    return out


def solution(mesh):
    placed = (P("gx", "gy", "gz"), P("gx", "gy", "gz"), P("gx", "gy", "gz"), P())
    return jax.shard_map(
        per_device, mesh=mesh, in_specs=placed, out_specs=P("gx", "gy", "gz"), check_vma=False
    )
```

```python
import jax
import jax.numpy as jnp
from jax import lax
from jax.experimental import pallas as pl
from jax.experimental.pallas import tpu as pltpu
from jax.sharding import PartitionSpec as P

SMOOTH_DEG = 4
COARSE_DEG = 8
SHIFT = 0.0005
SMOOTH = (0.5, 2.0)
COARSE = (0.1, 2.0)
F32 = jnp.float32
HIGHEST = lax.Precision.HIGHEST


def factors(degree, low, high):
    centre, half = (high + low) / 2.0, (high - low) / 2.0
    ratio = centre / half
    factor = 1.0 / ratio
    pairs = [(0.0, 1.0 / centre)]
    for _ in range(1, degree):
        following = 1.0 / (2.0 * ratio - factor)
        pairs.append((following * factor, 2.0 * following / half))
        factor = following
    return pairs


def lanes_like(shape):
    return lax.broadcasted_iota(jnp.int32, shape, len(shape) - 1)


def rows_like(shape):
    return lax.broadcasted_iota(jnp.int32, shape, len(shape) - 2)


def turn(v, by, axis):
    by = by % v.shape[axis]
    return v if by == 0 else pltpu.roll(v, by, axis)


def across(own, lane):
    up = [turn(v, 1, 1) for v in own]
    down = [turn(v, -1, 1) for v in own]
    if len(own) == 2:
        up = [jnp.where(lane == 0, up[1 - h], up[h]) for h in range(2)]
        down = [jnp.where(lane == 127, down[1 - h], down[h]) for h in range(2)]
    return [p + q for p, q in zip(up, down)]


def put(x, i, h, row, value, height, cyclic):
    x[i, h, pl.ds(8 + row, 8)] = value
    if cyclic and row == 0:
        x[i, h, pl.ds(8 + height, 1)] = value[0:1]
    if cyclic and row == height - 8:
        x[i, h, pl.ds(7, 1)] = value[7:8]


def stencil(x, first, group, halves, rows, use, flush=None):
    lane = lanes_like((8, 128))
    for row in rows:
        def load(i):
            return [x[i, h, pl.ds(8 + row, 8)] for h in range(halves)]

        below, own = load(first - 1), load(first)
        for j in range(group):
            i = first + j
            above = load(i + 1)
            side = across(own, lane)
            total = [
                (below[h] + above[h]) + (x[i, h, pl.ds(7 + row, 8)] + x[i, h, pl.ds(9 + row, 8)]) + side[h]
                for h in range(halves)
            ]
            use(j, row, own, total)
            below, own = own, above
        if flush is not None and (group > 4 or row // 8 % 2 == 1 or row == rows[-1]):
            flush()


def sweep(xin, xout, upd, src, inv, start, stop, a, c, group, cyclic, offset=0):
    halves, height = src.shape[1], src.shape[2]

    def body(first):
        def use(j, row, own, total):
            i, tile = first + j, pl.ds(row, 8)
            for h in range(halves):
                g = (src[i + offset, h, tile] + total[h]) * inv[i + offset, h, tile] - own[h]
                u = c * g if a == 0.0 else a * upd[i, h, tile] + c * g
                made.append((i, h, row, u, own[h] + u))

        def flush():
            for i, h, row, u, value in made:
                upd[i, h, pl.ds(row, 8)] = u
                put(xout, i, h, row, value, height, cyclic)
            made.clear()

        made = []
        stencil(xin, first, group, halves, range(0, height, 8), use, flush)

    steps = (stop - start) // group
    if steps == 1:
        body(start)
    else:
        def step(n, carry):
            body(start + n * group)
            return carry

        lax.fori_loop(0, steps, step, 0)


def dot(a, b):
    return lax.dot_general(a, b, (((1,), (0,)), ((), ())), precision=HIGHEST, preferred_element_type=F32)


def inverse(mass):
    return jnp.where(mass > 0.0, 1.0 / (6.0 + mass), 0.0)


def by_parity(place, a, b, body):
    odd = place[0] % 2
    pl.when(odd == 1)(lambda: body(a, b))
    pl.when(odd == 0)(lambda: body(b, a))


def first_kernel(table, pred, right, zone, main, to_next, to_before, codes, sems):
    moves = ((zone, codes), (pred, main.at[0]), (right, main.at[1]))
    copies = [pltpu.make_async_copy(*move, sems.at[n]) for n, move in enumerate(moves)]
    for copy in copies:
        copy.start()
    copies[0].wait()
    lane = lanes_like((32, 128))
    for x in range(8):
        code = codes[x]
        absorb = jnp.zeros((32, 128), F32)
        for k in range(16):
            absorb = absorb + jnp.where(code == k, table[k], 0.0)
        main[2, x] = SHIFT + absorb
    copies[1].wait()
    copies[2].wait()
    for edge, out in ((120, to_next), (0, to_before)):
        for half, fields in ((0, (0, 1)), (1, (2,))):
            packed = jnp.zeros((32, 128), F32)
            for n, f in enumerate(fields):
                for x in range(8):
                    at = 64 * n + 8 * x
                    moved = turn(main[f, x], at - edge, 1)
                    packed = jnp.where((lane >= at) & (lane < at + 8), moved, packed)
            out[half] = packed


def second_kernel(py, main, zbefore, znext, ya, yb, kept):
    kept[...] = main[...]

    def body(to_next, to_before):
        for start, out in ((24, to_next), (0, to_before)):
            rows = pl.ds(start, 8)
            for f in range(3):
                for x in range(8):
                    out[f * 8 + x] = main[f, x, rows]
            for half in range(2):
                out[24 + half] = zbefore[half, rows]
                out[26 + half] = znext[half, rows]

    by_parity(py, ya, yb, body)


def main_tile(f, k, t):
    return 4 * k + t + (f > 0) * (32 + 28 * (f - 1))


def y_tile(f, k):
    return 88 + 10 * f + (2 * k if k < 3 else 3 + k)


TILES = 142


def third_kernel(px, py, main, zbefore, znext, ya, yb, xa, xb, ybefore, ynext):
    row = rows_like((8, 128))

    def settle(after, before):
        ynext[...] = after[...]
        ybefore[...] = before[...]

    by_parity(py, ya, yb, settle)

    def body(to_next, to_before):
        for out in (to_next, to_before):
            for k in range(8):
                x = 7 - k if out is to_next else k
                for f in range(3 if k < 7 else 1):
                    for t in range(4):
                        out[main_tile(f, k, t)] = main[f, x, pl.ds(8 * t, 8)]
                    n, at = f * 8 + x, y_tile(f, k)
                    if k < 3:
                        out[at] = ynext[n]
                        out[at + 1] = ybefore[n]
                    elif k < 7:
                        out[at] = jnp.where(row < 4, ynext[n], ybefore[n])
            for half in range(2):
                for t in range(4):
                    out[118 + half * 4 + t] = zbefore[half, pl.ds(8 * t, 8)]
                    out[126 + half * 4 + t] = znext[half, pl.ds(8 * t, 8)]
            out[134:138] = ynext[24:28]
            out[138:142] = ybefore[24:28]

    by_parity(px, xa, xb, body)


def coarsen_matrix(source):
    rows = lax.broadcasted_iota(jnp.int32, (128, 128), 0)
    cols = lax.broadcasted_iota(jnp.int32, (128, 128), 1)
    return jnp.where(source(rows) == cols, 0.5, 0.0).astype(F32)


def descend_kernel(px, main, zbefore, znext, ybefore, ynext, xa, xb, fa, src, inv, one_out, give, keep,
                   fb, upd, mass, pair):
    lane = lanes_like((8, 128))
    row = rows_like((8, 128))
    zero = jnp.zeros((8, 128), F32)

    def own_tile(f, x, t):
        half = f // 2
        if 1 <= t < 5:
            tile = pl.ds(8 * t - 8, 8)
            return main[f, x, tile], zbefore[half, tile], znext[half, tile]
        side = ynext if t == 5 else ybefore
        return side[f * 8 + x], side[24 + half], side[26 + half]

    def far_tile(message, f, k, t):
        half = f // 2
        if 1 <= t < 5:
            return message[main_tile(f, k, t - 1)], message[118 + half * 4 + t - 1], message[126 + half * 4 + t - 1]
        at, corner = y_tile(f, k), 134 if t == 5 else 138
        if k < 3:
            centre = message[at + (t == 0)]
        elif k < 7:
            centre = jnp.where((row < 4) == (t == 5), message[at], 0.0)
        else:
            centre = zero
        return centre, message[corner + half], message[corner + 2 + half]

    def fill(planes, tile_of):
        for plane in planes:
            x = plane % 8
            for h in range(2):
                for field in (fa, fb):
                    field[plane, h, pl.ds(0, 8)] = zero
                    field[plane, h, pl.ds(56, 8)] = zero
            for f in range(3 if 0 < plane < 23 else 1):
                at = (f % 2) * 64 + 8 * x
                for t in range(6):
                    centre, zb, zn = tile_of(f, x, t)
                    side = jnp.where(lane < 8, turn(zn, -at, 1), 0.0)
                    side = jnp.where(lane >= 120, turn(zb, 120 - at, 1), side)
                    if f == 2:
                        if 8 <= plane < 16 and 1 <= t < 5:
                            mass[x, pl.ds(8 * t - 8, 8)] = centre
                        centre, side = inverse(centre), inverse(side)
                    dest, down = ((fa, 8), (src, 0), (inv, 0))[f]
                    dest[plane, 0, pl.ds(8 * t + down, 8)] = centre
                    dest[plane, 1, pl.ds(8 * t + down, 8)] = side

    fill(range(8, 16), own_tile)

    def fill_far(after, before):
        fill(range(8), lambda f, x, t: far_tile(before, f, 7 - x, t))
        fill(range(16, 24), lambda f, x, t: far_tile(after, f, x, t))

    by_parity(px, xa, xb, fill_far)
    xin, xout = fa, fb
    for k, (a, c) in enumerate(factors(SMOOTH_DEG, *SMOOTH)):
        sweep(xin, xout, upd, src, inv, k + 1, 23 - k, a, c, 11 - k, False)
        xin, xout = xout, xin
    def residual(j, row, own_tile, total):
        if 8 <= row < 40:
            tile = pl.ds(row - 8, 8)
            res = (src[8 + j, 0, pl.ds(row, 8)] + total[0]) - (6.0 + mass[j, tile]) * own_tile[0]
            if j % 2 == 0:
                held[row] = res
            else:
                pair[j // 2, tile] = held[row] + res
                pair[4 + j // 2, tile] = mass[j - 1, tile] + mass[j, tile]

    held = {}
    stencil(xin, 8, 8, 2, range(8, 40, 8), residual)
    even = pair[:, pl.ds(0, 16, stride=2), :] + pair[:, pl.ds(1, 16, stride=2), :]
    one = dot(even.reshape(128, 128), coarsen_matrix(lambda r: r // 2)).reshape(2, 4, 16, 128)
    one_out[...] = one
    lane = lanes_like((16, 128))

    def pack(to_next, to_before):
        for edge, out in ((32, to_next), (0, to_before)):
            for f in range(2):
                packed = jnp.zeros((16, 128), F32)
                for i in range(4):
                    packed = jnp.where(lane // 32 == i, turn(one[f, i], 32 * i - edge, 1), packed)
                out[f] = packed

    by_parity(px, give, keep, pack)


def widen_kernel(one, halo, out):
    lane = lanes_like((16, 128))
    for f in range(2):
        for i in range(4):
            v = one[f, i]
            v = jnp.where(lane // 32 == 2, turn(halo[0, f], 64 - 32 * i, 1), v)
            out[0, f, i] = jnp.where(lane // 32 == 3, turn(halo[1, f], 96 - 32 * i, 1), v)


def rows_kernel(py, near, ya, yb):
    def body(to_next, to_before):
        for start, extra, out in ((8, 7, to_next), (0, 8, to_before)):
            for n in range(32):
                block = near.at[n // 4 % 4, n // 16, n % 4]
                out[n] = block[pl.ds(start, 8)]
                out[32 + n // 8, pl.ds(n % 8, 1)] = block[pl.ds(extra, 1)]

    by_parity(py, ya, yb, body)


def join_kernel(py, near, ya, yb, out):
    row = rows_like((8, 128))

    def body(ynext, ybefore):
        for n in range(32):
            place = n // 4 % 4, n // 16, n % 4
            tile, at = 32 + n // 8, pl.ds(n % 8, 1)
            out[(*place, pl.ds(0, 16))] = near[place]
            out[(*place, pl.ds(16, 8))] = ynext[n]
            mix = jnp.where(row == 0, ynext[tile, at], 0.0)
            out[(*place, pl.ds(24, 8))] = jnp.where(row == 7, ybefore[tile, at], mix)
            out[(*place, pl.ds(32, 8))] = ybefore[n]

    by_parity(py, ya, yb, body)


def middle_kernel(place, near, far, fb, src, inv, two_out, edge_out,
                  fa, upd, mass, pair, pairs):
    zero = jnp.zeros((40, 128), F32)
    for end in (0, 1, 2, 3, 4, 5, 6, 39, 40, 41, 42, 43, 44, 45, 46):
        for field in (fa, fb):
            field[end, 0, pl.ds(8, 40)] = zero
        src[end, 0] = zero
        inv[end, 0] = zero
    (_, scale), *later = factors(SMOOTH_DEG, *SMOOTH)
    lane = lanes_like((40, 128))

    def fill(first, second):
        for j in range(4):
            group = (place[0] // 2 * 2) ^ ((j & 1) * 4 + (j >> 1) * 2)
            for i in range(4):
                pairs = []
                for f in range(2):
                    p, q = first[j, f, i], second[j, f, i]
                    v = jnp.where(lane < 96, turn(q, -32, 1), turn(p, 32, 1))
                    pairs.append((jnp.where(lane < 64, p, v), jnp.where(lane < 96, q, p)))
                for core in range(2):
                    plane = 7 + 4 * group + 4 * core + i
                    b1, m1 = pairs[0][core], pairs[1][core]
                    inv1 = inverse(m1)
                    mass[plane] = m1
                    src[plane, 0] = b1
                    inv[plane, 0] = inv1
                    u = scale * (b1 * inv1)
                    upd[plane, 0] = u
                    for t in range(5):
                        put(fa, plane, 0, 8 * t, u[8 * t:8 * t + 8], 40, True)

    by_parity(place, far, near, fill)
    xin, xout = fa, fb
    for a, c in later:
        sweep(xin, xout, upd, src, inv, 7, 39, a, c, 8, True)
        xin, xout = xout, xin

    def step(n, carry):
        def residual(j, row, own, total):
            p, tile = 7 + 4 * n + j, pl.ds(row, 8)
            res = (src[p, 0, tile] + total[0]) - (6.0 + mass[p, tile]) * own[0]
            if j % 2 == 0:
                held[row] = res
            else:
                pair[2 * n + j // 2, tile] = held[row] + res
                pair[16 + 2 * n + j // 2, tile] = mass[p - 1, tile] + mass[p, tile]

        held = {}
        stencil(xin, 7 + 4 * n, 4, 1, range(0, 40, 8), residual)
        return carry

    lax.fori_loop(0, 8, step, 0)
    even = pair[:, pl.ds(0, 20, stride=2), :] + pair[:, pl.ds(1, 20, stride=2), :]
    pairs[:, pl.ds(0, 20)] = even
    pairs[:, pl.ds(20, 4)] = jnp.zeros((32, 4, 128), F32)
    down = [coarsen_matrix(lambda r, h=h: 64 * h + 16 + jnp.where(r < 96, r // 2, r // 2 - 64)) for h in range(2)]
    for f in range(2):
        low = pairs[pl.ds(16 * f, 8)].reshape(192, 128)
        high = pairs[pl.ds(16 * f + 8, 8)].reshape(192, 128)
        made = (dot(low, down[0]) + dot(high, down[1])).reshape(8, 24, 128)
        for i in range(8):
            n = 8 * f + i
            two_out[n] = made[i, 0:8]
            edge_out[n] = made[i, 0:8]
            beyond = jnp.where(place[0] % 2 == 0, made[i, 18:20], made[i, 8:10])
            edge_out[16 + n // 4, pl.ds(2 * (n % 4), 2)] = beyond


def double(x, i, h, row, value):
    for odd in range(2):
        x.at[i, h][pl.ds(row + odd, value.shape[0], stride=2), :] = value


def one_hot(shape, axis, source):
    at = lax.broadcasted_iota(jnp.int32, shape, axis)
    return jnp.where(at == source, 1.0, 0.0).astype(F32)


def ascend_kernel(place, two, brought, given, x1, src1, inv1, x0, src0, inv0, out,
                  ca, cb, cupd, csrc, cinv, flat, oa, ob, oupd, za, zb, zupd):
    row = rows_like((8, 128))
    lane = lanes_like((32, 128))
    (_, scale), *later = factors(COARSE_DEG, *COARSE)

    def fill(after, before):
        for i in range(8):
            values = []
            for f in range(2):
                n = 8 * f + i
                mix = jnp.where(row < 2, turn(after[16 + n // 4], -2 * (n % 4), 0), 0.0)
                mix = jnp.where(row >= 6, turn(before[16 + n // 4], 6 - 2 * (n % 4), 0), mix)
                values.append(jnp.concatenate([two[n], after[n], mix, before[n]], axis=0))
            values[1] = inverse(values[1])
            csrc[1 + i, 0] = values[0]
            cinv[1 + i, 0] = values[1]
            u = scale * (values[0] * values[1])
            cupd[1 + i, 0] = u
            for t in range(4):
                put(ca, 1 + i, 0, 8 * t, u[8 * t:8 * t + 8], 32, True)

    by_parity(place, brought, given, fill)
    xin, xout = ca, cb
    core = pl.ds(8, 32)
    for a, c in later:
        xin[0, 0, core] = jnp.where(lane >= 64, pltpu.roll(xin[8, 0, core], 64, 1), 0.0)
        xin[9, 0, core] = jnp.where(lane < 64, pltpu.roll(xin[1, 0, core], 64, 1), 0.0)
        sweep(xin, xout, cupd, csrc, cinv, 1, 9, a, c, 8, True)
        xin, xout = xout, xin
    zero = jnp.zeros((32, 128), F32)
    for end in (0, 1, 2, 19, 20, 21):
        flat[end] = zero
    for q in range(16):
        v = xin[1 + q % 8, 0, core]
        flat[3 + q] = v if q < 8 else pltpu.roll(v, 64, 1)
    l = lax.broadcasted_iota(jnp.int32, (1, 128), 1)
    wide = one_hot((128, 128), 0, jnp.where(l < 96, 16 + l // 2, l // 2 - 48))
    part = dot(flat[pl.ds(2 * place[0], 8)].reshape(256, 128), wide)
    first = 4 * place[0] + 1
    for v in range(8):
        double(oa, 2 * v, 0, 32, part[32 * v + 24:32 * v + 32])
        double(oa, 2 * v, 0, 8, part[32 * v:32 * v + 14])
        for t in range(5):
            fine = oa[2 * v, 0, pl.ds(8 + 8 * t, 8)]
            for w in (2 * v, 2 * v + 1):
                put(oa, w, 0, 8 * t, x1[first + w, 0, pl.ds(8 + 8 * t, 8)] + fine, 40, True)
    xin, xout = oa, ob
    for k, (a, c) in enumerate(factors(SMOOTH_DEG, *SMOOTH)):
        sweep(xin, xout, oupd, src1, inv1, k + 1, 15 - k, a, c, 14 - 2 * k, True, offset=first)
        xin, xout = xout, xin
    side = jnp.where((l < 8) | (l >= 120), 64 + l // 2, -1)
    wide = [one_hot((128, 128), 0, l // 2), one_hot((128, 128), 0, side)]
    below = xin[4:12, 0, 8:48].reshape(320, 128)
    zero = jnp.zeros((8, 128), F32)
    for h in range(2):
        part = dot(below, wide[h])
        for v in range(8):
            double(za, 2 * v, h, 0, part[40 * v + 32:40 * v + 40])
            double(za, 2 * v, h, 16, part[40 * v:40 * v + 20])
            for t in range(6):
                tile = pl.ds(8 + 8 * t, 8)
                fine = za[2 * v, h, tile]
                for w in (2 * v, 2 * v + 1):
                    za[w, h, tile] = x0[4 + w, h, tile] + fine
            for w in (2 * v, 2 * v + 1):
                for field in (za, zb):
                    field[w, h, pl.ds(0, 8)] = zero
                    field[w, h, pl.ds(56, 8)] = zero
    xin, xout = za, zb
    for k, (a, c) in enumerate(factors(SMOOTH_DEG, *SMOOTH)):
        sweep(xin, xout, zupd, src0, inv0, k + 1, 15 - k, a, c, 7 - k, False, offset=4)
        xin, xout = xout, xin
    out[...] = xin[4:12, 0, 16:48]


def call(kernel, outs, scratch, *args, spaces=(), limit=24):
    vmem = pl.BlockSpec(memory_space=pltpu.VMEM)
    spaces = [pl.BlockSpec(memory_space=space) for space in spaces]
    scratch = [pltpu.VMEM(s, F32) if isinstance(s, tuple) else s for s in scratch]
    return pl.pallas_call(
        kernel,
        out_shape=[jax.ShapeDtypeStruct(s, F32) for s in outs],
        in_specs=spaces + [vmem] * (len(args) - len(spaces)),
        out_specs=[vmem] * len(outs),
        scratch_shapes=scratch,
        compiler_params=pltpu.CompilerParams(vmem_limit_bytes=limit * 1024 * 1024),
    )(*args)


def shift(value, axis, by):
    count = lax.axis_size(axis)
    pairs = [(i, i + by) for i in range(count) if 0 <= i + by < count]
    return lax.ppermute(value, axis, pairs)


def swap(value, axis, bit):
    return lax.ppermute(value, axis, [(i, i ^ bit) for i in range(lax.axis_size(axis))])


def swap_both(a, b, axis):
    count = lax.axis_size(axis)
    got = []
    for value, first in ((a, 1), (b, 0)):
        ups = [(i, i + 1) for i in range(first, count - 1, 2)]
        got.append(lax.ppermute(value, axis, ups + [(j, i) for i, j in ups]))
    return got


def cross(value, axis):
    count = lax.axis_size(axis)
    pairs = []
    for g in range(lax.axis_size("gx")):
        by = 1 - 2 * (g % 2)
        pairs += [(g * count + i, g * count + i + by) for i in range(count) if 0 <= i + by < count]
    return lax.ppermute(value, ("gx", axis), pairs)


def per_device(right_side, predicted, zone, zone_table):
    px = lax.axis_index("gx").astype(jnp.int32).reshape(1)
    py = lax.axis_index("gy").astype(jnp.int32).reshape(1)
    one_scalar, two_scalars = [pltpu.SMEM], [pltpu.SMEM] * 2
    block = (8, 32, 128)
    main, nxt, bef = call(first_kernel, [(3, *block), (2, 32, 128), (2, 32, 128)],
                          [pltpu.VMEM(block, jnp.int32), pltpu.SemaphoreType.DMA((3,))],
                          zone_table, predicted, right_side, zone,
                          spaces=[pltpu.SMEM, pltpu.HBM, pltpu.HBM, pltpu.HBM], limit=56)
    zbefore, znext = shift(nxt, "gz", 1), shift(bef, "gz", -1)
    ya, yb, main = call(second_kernel, [(28, 8, 128)] * 2 + [(3, *block)], [],
                        py, main, zbefore, znext, spaces=one_scalar)
    ya, yb = swap_both(ya, yb, "gy")
    xa, xb, ybefore, ynext = call(third_kernel, [(TILES, 8, 128)] * 2 + [(28, 8, 128)] * 2, [],
                                  px, py, main, zbefore, znext, ya, yb, spaces=two_scalars)
    xa, xb = swap_both(xa, xb, "gx")
    tall, flat = (24, 2, 64, 128), (24, 2, 48, 128)
    x0, src0, inv0, one, give, keep = call(
        descend_kernel,
        [tall, flat, flat, (2, 4, 16, 128), (2, 16, 128), (2, 16, 128)],
        [tall, flat, block, block],
        px, main, zbefore, znext, ybefore, ynext, xa, xb, spaces=one_scalar)
    halo = cross(jnp.stack([keep, swap(give, "gx", 1)]), "gz")
    near, = call(widen_kernel, [(1, 2, 4, 16, 128)], [], one, halo)
    near = jnp.concatenate([near, swap(near, "gx", 4)])
    near = jnp.concatenate([near, swap(near, "gx", 2)])
    ya, yb = call(rows_kernel, [(36, 8, 128)] * 2, [], py, near, spaces=one_scalar)
    ya, yb = swap_both(ya, yb, "gy")
    near, = call(join_kernel, [(4, 2, 4, 40, 128)], [], py, near, ya, yb, spaces=one_scalar)
    far = swap(near, "gx", 1)
    tall, flat = (47, 1, 56, 128), (47, 1, 40, 128)
    x1, src1, inv1, two, edge = call(
        middle_kernel,
        [tall, flat, flat, (16, 8, 128), (20, 8, 128)],
        [tall, flat, (47, 40, 128), (32, 40, 128), (32, 24, 128)],
        px, near, far, spaces=one_scalar)
    brought = cross(edge, "gy")
    given = swap(brought, "gx", 1)
    out, = call(
        ascend_kernel,
        [(8, 32, 128)],
        [(10, 1, 48, 128)] * 2 + [(10, 1, 32, 128)] * 3 + [(22, 32, 128)]
        + [(16, 1, 56, 128)] * 2 + [(16, 1, 40, 128)] + [(16, 2, 64, 128)] * 2 + [(16, 2, 48, 128)],
        px, two, brought, given, x1, src1, inv1, x0, src0, inv0, spaces=one_scalar)
    return out


def solution(mesh):
    placed = (P("gx", "gy", "gz"), P("gx", "gy", "gz"), P("gx", "gy", "gz"), P())
    return jax.shard_map(
        per_device, mesh=mesh, in_specs=placed, out_specs=P("gx", "gy", "gz"), check_vma=False
    )
```
